256 devices in a mesh: gossip: 32 (over y, z_hi, core), mp: 8 (over z_lo, x).
Axes of the slice: x: 4, y: 4, z: 8 (z_hi: 4, z_lo: 2; z = z_hi * 2 + z_lo), core: 2. Of those that a mesh axis runs over, the one named last changes fastest.
Arguments:
- params: float32 [32, 1024, 4096], P('gossip', None, 'mp'), may hold values from -6 to 6
- public: float32 [32, 1024, 64], P('gossip'), may hold values from -12 to 12
- gradients: bfloat16 [2, 32, 1024, 4096], P(None, 'gossip', None, 'mp'), may hold values from -130 to 130
- projection: float32 [4096, 64], P('mp'), may hold values from -0.09375 to 0.09375
- partners: int32 [2, 32], P(None, 'gossip'), may hold values from 0 to 31, as said below
Outputs:
- params_out: float32 [32, 1024, 4096], P('gossip', None, 'mp')
- public_out: float32 [32, 1024, 64], P('gossip')
- consensus: float32 [2], replicated
- grad_norm: float32 [2], replicated
The draws below stay inside these ranges and needn't reach their ends.
Inputs may be any that keep to these rules, and one draw needn't show every extreme that they name: Each row is a pairing of the 32 replicas: partners[r, partners[r, i]] = i and partners[r, i] != i.
All inputs are finite; a program needn't handle non-finite values.
Results may differ from the reference program's by a relative error of at most 0.008.
Values may be sent and summed in bfloat16 or wider, within the bound.
No kernel may reach another device: no remote copies, remote signals or barrier semaphores. Data moves between devices by JAX's collectives and lax.ppermute only.
A program may use at most 64 MiB of HBM per device.

```python
import math
import jax
import jax.numpy as jnp
from jax import lax

SLAB = 4096
RANK = 64
ROWS = 1024
ROUNDS = 2
NODES = 32


def draw_gradients(key, part):
    keys = jax.random.split(key, 5)
    shape = (ROUNDS, NODES, ROWS, SLAB)
    row_scale = jnp.exp(jax.random.uniform(keys[0], (ROUNDS, NODES, ROWS, 1), jnp.float32, math.log(0.3), math.log(3.0)))
    col_scale = jnp.exp(jax.random.uniform(keys[1], (ROUNDS, 1, 1, SLAB), jnp.float32, math.log(0.3), math.log(3.0)))
    node_scale = jnp.exp(jnp.linspace(0.0, math.log(3.0), NODES)).reshape(1, NODES, 1, 1)
    base = jnp.clip(jax.random.normal(keys[4], shape, jnp.float32), -4.0, 4.0)
    return (base * row_scale * col_scale * node_scale).astype(jnp.bfloat16)


def draw_public(key, part):
    keys = jax.random.split(key, 3)
    shape = (NODES, ROWS, RANK)
    node_scale = jnp.exp(jnp.linspace(0.0, math.log(3.0), NODES)).reshape(NODES, 1, 1)
    base = jnp.clip(jax.random.normal(keys[2], shape, jnp.float32), -4.0, 4.0)
    return (base * node_scale).astype(jnp.float32)


def draw_partners(key, part):
    rows_list = []
    for round_index in range(ROUNDS):
        order = jax.random.permutation(jax.random.fold_in(key, 71 + round_index), NODES).astype(jnp.int32)
        first = order[0::2]
        second = order[1::2]
        paired = jnp.zeros((NODES,), jnp.int32).at[first].set(second).at[second].set(first)
        rows_list.append(paired)
    return jnp.stack(rows_list)


def steps_of(key, dims, pieces, least, high):
    factor_of = 1.0
    for axis_at, blocks in pieces:
        draws = jax.random.uniform(jax.random.fold_in(jax.random.fold_in(key, 6), axis_at), (blocks,), jnp.float32, least / len(pieces), high / len(pieces))
        factor_of = factor_of * jnp.repeat(jnp.exp(draws), dims[axis_at] // blocks).reshape((-1,) + (1,) * (len(dims) - 1 - axis_at))
    return factor_of


def normal_values(own_key, dims, deviation, reach, cuts=(), kind=jnp.bfloat16):
    drawn = jax.random.normal(own_key, dims, jnp.float32) * deviation
    if len(cuts) > 0:
        drawn = steps_of(own_key, dims, cuts, -0.22, 0.18) * drawn
    return jnp.clip(drawn, min=-reach, max=reach).astype(kind)


def setup_inputs(seed: int = 0) -> dict:
    arg_keys = jax.random.split(jax.random.key(seed), 6)
    return {
        "params": normal_values(arg_keys[0], (NODES, ROWS, SLAB), 1.0, 6.0, ((0, 32), (2, 8)), jnp.float32),
        "public": draw_public(jax.random.fold_in(arg_keys[5], 71), 0),
        "gradients": draw_gradients(jax.random.fold_in(arg_keys[5], 71), 0),
        "projection": normal_values(arg_keys[3], (SLAB, RANK), SLAB ** -0.5, 0.09375, ((0, 8),), jnp.float32),
        "partners": draw_partners(jax.random.fold_in(arg_keys[5], 71), 0),
    }


step_size = 1.0
clip_limit = 0.5
mixing = 0.4
epsilon = 1e-06

def reference(params, public, gradients, projection, partners):
    highest = lax.Precision.HIGHEST
    total = NODES * ROWS * SLAB
    weights = params
    public_state = public
    drift_list = []
    norm_list = []
    for round_index in range(ROUNDS):
        grad_round = gradients[round_index]
        squares = jnp.sum(lax.map(lambda block: jnp.sum(jnp.square(block.astype(jnp.float32))), grad_round))
        norm_value = jnp.sqrt(squares / total + epsilon)
        scale = jnp.minimum(1.0, clip_limit / norm_value)

        def coefficients(item):
            node_weights, node_grad, node_coef = item
            half = node_weights - step_size * scale * node_grad.astype(jnp.float32)
            rebuilt = jnp.dot(node_coef, projection.T, precision=highest)
            return node_coef + jnp.dot(half - rebuilt, projection, precision=highest)
        coef = lax.map(coefficients, (weights, grad_round, public_state))
        sent = coef.astype(jnp.bfloat16)
        mate = jnp.take(sent, partners[round_index], axis=0)
        public_state = sent.astype(jnp.float32)

        def blend(item):
            node_weights, node_grad, own_coef, other_coef = item
            half = node_weights - step_size * scale * node_grad.astype(jnp.float32)
            drift = jnp.dot(other_coef.astype(jnp.float32) - own_coef, projection.T, precision=highest)
            return (half + mixing * drift, jnp.sum(drift * drift))
        weights, terms = lax.map(blend, (weights, grad_round, public_state, mate))
        drift_list.append(jnp.sum(terms) / total)
        norm_list.append(norm_value)
    return (weights, public_state, jnp.stack(drift_list), jnp.stack(norm_list))
```

```python
import functools

import jax
import jax.numpy as jnp
from jax import lax
from jax.experimental import pallas as pl
from jax.experimental.pallas import tpu as pltpu
from jax.sharding import PartitionSpec as P

F32 = jnp.float32
BF16 = jnp.bfloat16
AXES = ("gossip", "mp")
HIGHEST = lax.Precision.HIGHEST

NODES = 32
MP = 8
ROWS = 1024
RANK = 64
SLAB = 4096
DEVICES = 256
QUARTER = ROWS // 4
TOTAL = NODES * ROWS * SLAB

step_size = 1.0
clip_limit = 0.5
mixing = 0.4
epsilon = 1e-06


def lanes(shape):
    return lax.broadcasted_iota(jnp.int32, shape, 1)


def split_two(x):
    hi = x.astype(BF16)
    return hi, (x - hi.astype(F32)).astype(BF16)


def dot(a, b, **kw):
    return jnp.dot(a, b, preferred_element_type=F32, **kw)


def project_kernel(part_ref, w_ref, g_ref, c_ref, p_ref, out_ref, rhs, acc, stage, gram, squares, misc):
    k = pl.program_id(0)
    me = lax.axis_index("gossip")
    col = lax.axis_index("mp")

    @pl.when(k == 0)
    def _():
        p = p_ref[...]
        hi, lo = split_two(p)
        zero = jnp.zeros_like(hi)
        rhs[0] = jnp.concatenate([hi, zero, lo, zero], axis=1)
        rhs[1] = jnp.concatenate([zero, hi, zero, lo], axis=1)
        both = jnp.concatenate([p, p], axis=1)
        gram[...] = lax.dot_general(
            p, both, (((0,), (0,)), ((), ())), precision=HIGHEST, preferred_element_type=F32
        )
        squares[...] = jnp.zeros_like(squares)

    right = rhs[k % 2]
    w_hi, w_lo = split_two(w_ref[0])
    whole = dot(w_hi, right)
    values = [whole[:, :128] + whole[:, 128:] + dot(w_lo, right[:, :128])]
    for r in range(2):
        g = g_ref[r, 0]
        whole = dot(g, right)
        values.append(whole[:, :128] + whole[:, 128:])
        gf = g.astype(F32)
        squares[r] += jnp.sum((gf * gf).reshape(QUARTER // 8, 8, -1), axis=0)

    @pl.when(k % 2 == 0)
    def _():
        for a in range(3):
            acc[a] = values[a]

    for half in range(2):

        @pl.when(k == 2 * half + 1)
        def _():
            for a in range(3):
                stage[pl.ds(2 * a + half, QUARTER, 8), :] = acc[a] + values[a]

    @pl.when(k == col // 2)
    def _():
        c = c_ref[0]
        hi = c.astype(BF16).astype(F32)
        own = jnp.where(col % 2 == 0, hi, c - hi)
        misc[...] = jnp.concatenate([own, jnp.zeros_like(own)], axis=1)

    @pl.when(k == 3)
    def _():
        lane = lanes((1, 128))
        row = jnp.where(lane < RANK, gram[pl.ds(me, 1), :], gram[pl.ds(me + 32, 1), :])
        stage[pl.ds(6, QUARTER, 8), :] = jnp.broadcast_to(row, (QUARTER, 128))
        extra = jnp.zeros((1, 128), F32)
        for r in range(2):
            total = jnp.sum(squares[r], axis=(0, 1), keepdims=True)
            hi = total.astype(BF16).astype(F32)
            extra = jnp.where(lane == 64 + 2 * r, hi, extra)
            extra = jnp.where(lane == 65 + 2 * r, total - hi, extra)
            extra = jnp.where(lane == 68 + r, part_ref[r, 0].astype(F32), extra)
        stage[pl.ds(7, QUARTER, 8), :] = misc[...] + extra
        out_ref[...] = stage[...].reshape(DEVICES, 8, 128).astype(BF16)


def mix_kernel(in_ref, piece_ref, vec_ref, norm_ref, stage):
    stage[...] = in_ref[...].astype(F32).reshape(DEVICES * 8, 128)

    def loaded(m, j):
        return stage[pl.ds(8 * m + j, NODES, 8 * MP), :]

    def summed(j):
        return functools.reduce(lambda a, b: a + b, [loaded(m, j) for m in range(MP)])

    proj, back0, back1 = [
        jnp.concatenate([summed(2 * a), summed(2 * a + 1)], axis=1) for a in range(3)
    ]
    extras = [loaded(m, 7) for m in range(MP)]
    start = jnp.concatenate(
        [extras[2 * k][:, :RANK] + extras[2 * k + 1][:, :RANK] for k in range(4)], axis=1
    )
    lane = lanes((NODES, 128))
    every = functools.reduce(lambda a, b: a + b, extras)
    scales = []
    for r in range(2):
        chosen = (lane == 64 + 2 * r) | (lane == 65 + 2 * r)
        total = jnp.sum(jnp.where(chosen, every, 0.0), axis=(0, 1), keepdims=True)
        norm = jnp.sqrt(total / TOTAL + epsilon)
        scales.append(step_size * jnp.minimum(1.0, clip_limit / norm))
        norm_ref[r] = norm[0, 0]
    pairing = []
    for r in range(2):
        mate = jnp.sum(jnp.where(lane == 68 + r, extras[0], 0.0), axis=1, keepdims=True)
        column = lanes((NODES, NODES)).astype(F32)
        pairing.append(jnp.where(column == mate, 1.0, 0.0).astype(BF16))

    rows = summed(6)
    turned = pltpu.roll(rows, RANK, 1)
    twice = jnp.concatenate(
        [jnp.where(lane < RANK, rows, turned), jnp.where(lane < RANK, turned, rows)], axis=0
    )
    wide = jnp.concatenate([twice, twice], axis=1)
    tall = jnp.concatenate([wide] * 4, axis=0)
    square = (256, 256)
    same = lax.broadcasted_iota(jnp.int32, square, 0) // RANK == lanes(square) // RANK
    gram = jnp.where(same, tall, 0.0)

    def through(x):
        return dot(x, gram, precision=HIGHEST)

    stepped = proj - scales[0] * back0
    coef0 = start - through(start) + stepped
    sent0 = coef0.astype(BF16)
    own0 = sent0.astype(F32)
    drift0 = dot(pairing[0], sent0) - own0
    both = through(jnp.concatenate([drift0, own0], axis=0))
    moved0 = both[:NODES]
    coef1 = own0 - both[NODES:] + (stepped - scales[1] * back1) + mixing * moved0
    sent1 = coef1.astype(BF16)
    own1 = sent1.astype(F32)
    drift1 = dot(pairing[1], sent1) - own1
    moved1 = through(drift1)
    extra = jnp.zeros((NODES, 128), F32)
    for r, (d, moved) in enumerate(((drift0, moved0), (drift1, moved1))):
        total = jnp.sum(d * moved, axis=(0, 1), keepdims=True)
        hi = total.astype(BF16).astype(F32)
        extra = jnp.where(lane == 2 * r, hi, extra)
        extra = jnp.where(lane == 2 * r + 1, total - hi, extra)
    piece_ref[...] = jnp.concatenate(
        [drift0 + drift1, extra, own1, jnp.zeros((NODES, 128), F32)], axis=1
    ).astype(BF16)
    vec_ref[...] = jnp.concatenate(
        [jnp.broadcast_to(scales[0], (8, 128)), jnp.broadcast_to(scales[1], (8, 128))], axis=0
    )


def blend_kernel(in_ref, vec_ref, w_ref, g_ref, p_ref, out_ref, pub_ref, cons_ref, right):
    k = pl.program_id(0)

    @pl.when(k == 0)
    def _():
        hi, lo = split_two(p_ref[...].T)
        right[0] = jnp.concatenate([hi] * 4, axis=0)
        right[1] = jnp.concatenate([lo] * 4, axis=0)
        extra = in_ref[:, 256:384].astype(F32)
        lane = lanes((DEVICES, 128))
        for r in range(2):
            chosen = (lane == 2 * r) | (lane == 2 * r + 1)
            total = jnp.sum(jnp.where(chosen, extra, 0.0), axis=(0, 1), keepdims=True)
            cons_ref[r] = (total / TOTAL)[0, 0]

    square = (DEVICES, 256)
    mine = lanes(square) // RANK == k
    zero = jnp.zeros(square, BF16)
    moved = jnp.where(mine, in_ref[:, :256], zero)
    drift = dot(moved, right[0]) + dot(moved, right[1])
    scale0 = vec_ref[0:1, 0:1]
    scale1 = vec_ref[8:9, 0:1]
    half = w_ref[0] - scale0 * g_ref[0, 0].astype(F32) - scale1 * g_ref[1, 0].astype(F32)
    out_ref[0] = half + mixing * drift
    pick = (lax.broadcasted_iota(jnp.int32, (256, RANK), 0) % RANK == lanes((256, RANK))).astype(F32)
    sent = jnp.where(mine, in_ref[:, 384:640], zero)
    pub_ref[0] = dot(sent, pick.astype(BF16))


def body(params, public, gradients, projection, partners):
    width = params.shape[2]
    smem = pl.BlockSpec(memory_space=pltpu.SMEM)
    w_spec = pl.BlockSpec((1, QUARTER, width), lambda k: (0, k, 0))
    g_spec = pl.BlockSpec((2, 1, QUARTER, width), lambda k: (0, 0, k, 0))
    c_spec = pl.BlockSpec((1, QUARTER, RANK), lambda k: (0, k, 0))
    p_spec = pl.BlockSpec((width, RANK), lambda k: (0, 0))
    limit = pltpu.CompilerParams(vmem_limit_bytes=48 << 20)
    outgoing = pl.pallas_call(
        project_kernel,
        grid=(4,),
        out_shape=jax.ShapeDtypeStruct((DEVICES, 8, 128), BF16),
        in_specs=[smem, w_spec, g_spec, c_spec, p_spec],
        out_specs=pl.BlockSpec((DEVICES, 8, 128), lambda k: (0, 0, 0)),
        scratch_shapes=[
            pltpu.VMEM((2, width, 256), BF16),
            pltpu.VMEM((3, QUARTER, 128), F32),
            pltpu.VMEM((DEVICES * 8, 128), F32),
            pltpu.VMEM((RANK, 128), F32),
            pltpu.VMEM((2, 8, width), F32),
            pltpu.VMEM((QUARTER, 128), F32),
        ],
        compiler_params=limit,
    )(partners, params, gradients, public, projection)
    arrived = lax.all_to_all(outgoing, AXES, 0, 0, tiled=True)
    piece, scales, norms = pl.pallas_call(
        mix_kernel,
        out_shape=(
            jax.ShapeDtypeStruct((NODES, 768), BF16),
            jax.ShapeDtypeStruct((16, 128), F32),
            jax.ShapeDtypeStruct((2,), F32),
        ),
        out_specs=(
            pl.BlockSpec(memory_space=pltpu.VMEM),
            pl.BlockSpec(memory_space=pltpu.VMEM),
            smem,
        ),
        scratch_shapes=[pltpu.VMEM((DEVICES * 8, 128), F32)],
        compiler_params=limit,
    )(arrived)
    spread = jnp.broadcast_to(piece.reshape(NODES, 1, 2, 384), (NODES, MP, 2, 384))
    spread = spread.reshape(DEVICES, 2, 384)
    back = lax.all_to_all(spread, AXES, 0, 0, tiled=True).reshape(DEVICES, 768)
    weights, state, consensus = pl.pallas_call(
        blend_kernel,
        grid=(4,),
        out_shape=(
            jax.ShapeDtypeStruct(params.shape, F32),
            jax.ShapeDtypeStruct(public.shape, F32),
            jax.ShapeDtypeStruct((2,), F32),
        ),
        in_specs=[
            pl.BlockSpec((DEVICES, 768), lambda k: (0, 0)),
            pl.BlockSpec((16, 128), lambda k: (0, 0)),
            w_spec,
            g_spec,
            p_spec,
        ],
        out_specs=(w_spec, c_spec, smem),
        scratch_shapes=[pltpu.VMEM((2, 256, width), BF16)],
        compiler_params=limit,
    )(back, scales, params, gradients, projection)
    return weights, state, consensus, norms


def solution(mesh):
    placed = (
        P("gossip", None, "mp"),
        P("gossip", None, None),
        P(None, "gossip", None, "mp"),
        P("mp", None),
        P(None, "gossip"),
    )
    return jax.shard_map(
        body,
        mesh=mesh,
        in_specs=placed,
        out_specs=(P("gossip", None, "mp"), P("gossip", None, None), P(), P()),
        check_vma=False,
    )
```

```python
import functools

import jax
import jax.numpy as jnp
from jax import lax
from jax.experimental import pallas as pl
from jax.experimental.pallas import tpu as pltpu
from jax.sharding import Mesh
from jax.sharding import PartitionSpec as P

F32 = jnp.float32
BF16 = jnp.bfloat16
HIGHEST = lax.Precision.HIGHEST

NODES = 32
MP = 8
ROWS = 1024
RANK = 64
SLAB = 4096
DEVICES = NODES * MP
SHARE = ROWS // MP
CHUNKS = 4
CHUNK = ROWS // CHUNKS
FIRST = 208
PARTS = (("w", 0, 512), ("w", 512, 1024), ("g0", 0, 1024), ("g1", 0, 1024))
MP_ORDER = ("mp_1", "mp_0")
GOSSIP_ORDER = ("gossip_2", "gossip_0", "gossip_1")
BACK_ORDER = ("gossip_2", "mp_1", "mp_0", "gossip_0", "gossip_1")
PLANE = NODES // 2
TOTAL = NODES * ROWS * SLAB

step_size = 1.0
clip_limit = 0.5
mixing = 0.4
epsilon = 1e-06


def lanes(shape):
    return lax.broadcasted_iota(jnp.int32, shape, 1)


def rounded(x):
    return x.astype(BF16).astype(F32)


def split_two(x):
    hi = x.astype(BF16)
    return hi, (x - hi.astype(F32)).astype(BF16)


def dot(a, b, **kw):
    return jnp.dot(a, b, preferred_element_type=F32, **kw)


def project_kernel(w_hbm, g_hbm, c_hbm, p_hbm, out_ref, own_ref, w, g, c, p, gram, sems):
    me = lax.axis_index(GOSSIP_ORDER)
    first = pl.multiple_of(lax.axis_index(MP_ORDER) * SHARE, SHARE)
    p_copy = pltpu.make_async_copy(p_hbm, p, sems.at[len(PARTS)])
    p_copy.start()
    loads = []
    for i, (name, begin, end) in enumerate(PARTS):
        rows = pl.ds(begin, end - begin)
        if name == "w":
            copy = pltpu.make_async_copy(w_hbm.at[0, rows], w.at[rows], sems.at[i])
        else:
            r = int(name[1])
            copy = pltpu.make_async_copy(g_hbm.at[r, 0, rows], g.at[r, rows], sems.at[i])
        copy.start()
        loads.append(copy)
    c_copy = pltpu.make_async_copy(c_hbm.at[:, pl.ds(first, SHARE)], c, sems.at[len(PARTS) + 1])
    c_copy.start()
    p_copy.wait()
    low = lanes((64, 128)) < RANK
    pt = p[...]
    hi = rounded(pt)
    lo = rounded(pt - hi)
    right = jnp.concatenate([hi, hi, lo, lo], axis=0).T.astype(BF16)
    gram[...] = lax.dot_general(
        pt, jnp.concatenate([pt, pt], axis=0), (((1,), (1,)), ((), ())),
        precision=HIGHEST, preferred_element_type=F32,
    )
    lane = lanes((1, 128))
    row = jnp.where(lane < RANK, gram[pl.ds(me, 1), :], gram[pl.ds(me + NODES, 1), :])
    row_hi = rounded(row)
    scalars = jnp.zeros((1, 128), F32)
    for (name, begin, end), copy in zip(PARTS, loads):

        def store(a, value):
            for s in range((end - begin) // SHARE):
                at = s * SHARE
                packed = jnp.where(low, value[at : at + 64], value[at + 64 : at + 128])
                out_ref[begin // SHARE + s, 64 * a : 64 * a + 64, :] = packed.astype(BF16)

        copy.wait()
        if name == "w":
            w_hi, w_lo = split_two(w[begin:end, :])
            whole = dot(w_hi, right)
            store(0, whole[:, :128] + whole[:, 128:] + dot(w_lo, right[:, :128]))
        else:
            r = int(name[1])
            grad = g[r]
            whole = dot(grad, right)
            store(1 + r, whole[:, :128] + whole[:, 128:])
            gf = grad.astype(F32)
            squares = jnp.sum((gf * gf).reshape(ROWS // 8, 8, -1), axis=0)
            total = jnp.sum(squares, axis=(0, 1), keepdims=True)
            hi = rounded(total)
            scalars = jnp.where(lane == 2 * r, hi, scalars)
            scalars = jnp.where(lane == 2 * r + 1, total - hi, scalars)
    c_copy.wait()
    ct = c[...].T
    own_ref[...] = jnp.concatenate([ct[:64], ct[64:]], axis=1)
    at = lax.broadcasted_iota(jnp.int32, (16, 128), 0)
    extra = jnp.where(at == 0, row_hi, jnp.where(at == 1, row - row_hi, jnp.where(at == 2, scalars, 0.0)))
    extra = extra.astype(BF16)
    for m in range(MP):
        out_ref[m, 192:FIRST, :] = extra


def gather_kernel(part_ref, in_ref, own_ref, out_ref):
    value = in_ref[0].astype(F32)
    for m in range(1, MP):
        value += in_ref[m].astype(F32)

    def halves(x):
        return [x[:32], x[32:]]

    wide = (NODES, 128)
    row = value[192:193] + value[193:194]
    row_hi = rounded(row)
    lane = lanes((1, 128))
    pair = value[194:195]
    scalars = jnp.zeros((1, 128), F32)
    for r in range(2):
        chosen = (lane == 2 * r) | (lane == 2 * r + 1)
        total = jnp.sum(jnp.where(chosen, pair, 0.0), axis=1, keepdims=True)
        hi = rounded(total)
        scalars = jnp.where(lane == 2 * r, hi, scalars)
        scalars = jnp.where(lane == 2 * r + 1, total - hi, scalars)
        mate = part_ref[0, r]
        place = (mate % 2) * PLANE + mate // 2
        scalars = jnp.where(lane == 4 + r, place.astype(F32), scalars)
    upper = halves(value[:64]) + halves(value[64:128])
    upper += [jnp.broadcast_to(row_hi, wide), jnp.zeros(wide, F32)]
    lower = halves(value[128:192]) + halves(own_ref[...])
    lower += [jnp.broadcast_to(row - row_hi, wide), jnp.broadcast_to(scalars, wide)]
    out_ref[...] = jnp.stack(
        [jnp.concatenate(upper, axis=1), jnp.concatenate(lower, axis=1)], axis=1
    ).astype(BF16)


def mix_kernel(in_ref, piece_ref, vec_ref, norm_ref):
    value = in_ref[...].astype(F32)
    upper, lower = value[:, 0, :], value[:, 1, :]
    proj, back0 = upper[:, :256], upper[:, 256:512]
    back1, start = lower[:, :256], lower[:, 256:512]
    rows = upper[:, 512:640] + lower[:, 512:640]
    scalars = lower[:, 640:]
    lane = lanes((NODES, 128))
    scales = []
    for r in range(2):
        chosen = (lane == 2 * r) | (lane == 2 * r + 1)
        total = jnp.sum(jnp.where(chosen, scalars, 0.0), axis=(0, 1), keepdims=True)
        norm = jnp.sqrt(total / TOTAL + epsilon)
        scales.append(step_size * jnp.minimum(1.0, clip_limit / norm))
        norm_ref[r] = norm[0, 0]
    pairing = []
    for r in range(2):
        mate = jnp.sum(jnp.where(lane == 4 + r, scalars, 0.0), axis=1, keepdims=True)
        column = lanes((NODES, NODES)).astype(F32)
        pairing.append(jnp.where(column == mate, 1.0, 0.0).astype(BF16))

    turned = pltpu.roll(rows, RANK, 1)
    twice = jnp.concatenate(
        [jnp.where(lane < RANK, rows, turned), jnp.where(lane < RANK, turned, rows)], axis=0
    )
    wide = jnp.concatenate([twice, twice], axis=1)
    tall = jnp.concatenate([wide] * 4, axis=0)
    square = (256, 256)
    same = lax.broadcasted_iota(jnp.int32, square, 0) // RANK == lanes(square) // RANK
    gram = jnp.where(same, tall, 0.0)

    def through(x):
        return dot(x, gram, precision=HIGHEST)

    stepped = proj - scales[0] * back0
    coef0 = start - through(start) + stepped
    sent0 = coef0.astype(BF16)
    own0 = sent0.astype(F32)
    drift0 = dot(pairing[0], sent0) - own0
    both = through(jnp.concatenate([drift0, own0], axis=0))
    moved0 = both[:NODES]
    coef1 = own0 - both[NODES:] + (stepped - scales[1] * back1) + mixing * moved0
    sent1 = coef1.astype(BF16)
    own1 = sent1.astype(F32)
    drift1 = dot(pairing[1], sent1) - own1
    moved1 = through(drift1)
    extra = jnp.zeros((NODES, 128), F32)
    for r, (d, moved) in enumerate(((drift0, moved0), (drift1, moved1))):
        total = jnp.sum(d * moved, axis=(0, 1), keepdims=True)
        hi = rounded(total)
        extra = jnp.where(lane == 2 * r, hi, extra)
        extra = jnp.where(lane == 2 * r + 1, total - hi, extra)
    piece = jnp.stack(
        [
            jnp.concatenate([drift0 + drift1, extra], axis=1),
            jnp.concatenate([own1, jnp.zeros((NODES, 128), F32)], axis=1),
        ],
        axis=1,
    ).astype(BF16)
    for core in range(2):
        for m in range(MP):
            piece_ref[core, m] = piece[core * PLANE : (core + 1) * PLANE]
    vec_ref[...] = jnp.concatenate(
        [jnp.broadcast_to(scales[0], (8, 128)), jnp.broadcast_to(scales[1], (8, 128))], axis=0
    )


def step_kernel(vec_ref, w_ref, g_ref, p_ref, out_ref, right_ref):
    scale0 = vec_ref[0:1, 0:1]
    scale1 = vec_ref[8:9, 0:1]
    out_ref[...] = w_ref[0] - scale0 * g_ref[0, 0].astype(F32) - scale1 * g_ref[1, 0].astype(F32)

    @pl.when(pl.program_id(0) == 0)
    def _():
        hi, lo = split_two(p_ref[...])
        right_ref[0] = jnp.concatenate([hi] * 4, axis=0)
        right_ref[1] = jnp.concatenate([lo] * 4, axis=0)


def blend_kernel(in_ref, half_ref, right_ref, out_hbm, pub_ref, cons_ref, out, sems):
    square = (SHARE, 256)
    block = lax.broadcasted_iota(jnp.int32, square, 0) // NODES
    wanted = jnp.where(block == 1, 2, jnp.where(block == 2, 1, block))
    mine = lanes(square) // RANK == wanted
    zero = jnp.zeros(square, BF16)
    pick = (lax.broadcasted_iota(jnp.int32, (256, RANK), 0) % RANK == lanes((256, RANK))).astype(F32)
    pick = pick.astype(BF16)

    def spread(m, begin):
        rows = [
            in_ref[(core * MP + m) * PLANE : (core * MP + m + 1) * PLANE, begin : begin + 256]
            for core in range(2)
        ]
        return jnp.where(mine, jnp.concatenate(rows * 4, axis=0), zero)

    copies = []
    per = CHUNK // SHARE
    for k in range(CHUNKS):
        moved = jnp.concatenate([spread(k * per + s, 0) for s in range(per)], axis=0)
        drift = dot(moved, right_ref[0]) + dot(moved, right_ref[1])
        at = pl.ds(k * CHUNK, CHUNK)
        out[at, :] = half_ref[at, :] + mixing * drift
        copy = pltpu.make_async_copy(out.at[at], out_hbm.at[0, at], sems.at[k])
        copy.start()
        copies.append(copy)
    for k in range(CHUNKS):
        sent = jnp.concatenate([spread(k * per + s, 384) for s in range(per)], axis=0)
        pub_ref[0, :, k * CHUNK : (k + 1) * CHUNK] = lax.dot_general(
            pick, sent, (((0,), (1,)), ((), ())), preferred_element_type=F32
        )
    extra = in_ref[:, 256:384].astype(F32)
    lane = lanes((DEVICES, 128))
    for r in range(2):
        chosen = (lane == 2 * r) | (lane == 2 * r + 1)
        total = jnp.sum(jnp.where(chosen, extra, 0.0), axis=(0, 1), keepdims=True)
        cons_ref[r] = (total / TOTAL)[0, 0]
    for copy in copies:
        copy.wait()


def body(params, public, gradients, projection, partners):
    width = params.shape[2]
    smem = pl.BlockSpec(memory_space=pltpu.SMEM)
    vmem = pl.BlockSpec(memory_space=pltpu.VMEM)
    hbm = pl.BlockSpec(memory_space=pltpu.HBM)
    limit = pltpu.CompilerParams(vmem_limit_bytes=32 << 20)
    columns = projection.T
    stay = [pltpu.with_memory_space_constraint(x, pltpu.HBM) for x in (params, gradients, public[0].T, columns)]
    outgoing, own = pl.pallas_call(
        project_kernel,
        out_shape=(
            jax.ShapeDtypeStruct((MP, FIRST, 128), BF16),
            jax.ShapeDtypeStruct((64, 128), F32),
        ),
        in_specs=[hbm, hbm, hbm, hbm],
        out_specs=(vmem, vmem),
        scratch_shapes=[
            pltpu.VMEM((ROWS, width), F32),
            pltpu.VMEM((2, ROWS, width), BF16),
            pltpu.VMEM((RANK, SHARE), F32),
            pltpu.VMEM((RANK, width), F32),
            pltpu.VMEM((RANK, 128), F32),
            pltpu.SemaphoreType.DMA((len(PARTS) + 2,)),
        ],
        compiler_params=limit,
    )(*stay)
    arrived = lax.all_to_all(outgoing, MP_ORDER, 0, 0, tiled=True)
    outgoing = pl.pallas_call(
        gather_kernel,
        out_shape=jax.ShapeDtypeStruct((NODES, 2, 768), BF16),
        in_specs=[smem, vmem, vmem],
        out_specs=vmem,
        compiler_params=limit,
    )(partners.T, arrived, own)
    arrived = lax.all_to_all(outgoing, GOSSIP_ORDER, 0, 0, tiled=True)
    piece, scales, norms = pl.pallas_call(
        mix_kernel,
        out_shape=(
            jax.ShapeDtypeStruct((2, MP, PLANE, 2, 384), BF16),
            jax.ShapeDtypeStruct((16, 128), F32),
            jax.ShapeDtypeStruct((2,), F32),
        ),
        in_specs=[vmem],
        out_specs=(vmem, vmem, smem),
        compiler_params=limit,
    )(arrived)
    spread = piece.reshape(DEVICES, 2, 384)
    back = lax.all_to_all(spread, BACK_ORDER, 0, 0, tiled=True).reshape(DEVICES, 768)
    half, right = pl.pallas_call(
        step_kernel,
        grid=(CHUNKS,),
        out_shape=(
            jax.ShapeDtypeStruct((ROWS, width), F32),
            jax.ShapeDtypeStruct((2, 256, width), BF16),
        ),
        in_specs=[
            pl.BlockSpec((16, 128), lambda k: (0, 0)),
            pl.BlockSpec((1, CHUNK, width), lambda k: (0, k, 0)),
            pl.BlockSpec((2, 1, CHUNK, width), lambda k: (0, 0, k, 0)),
            pl.BlockSpec((RANK, width), lambda k: (0, 0)),
        ],
        out_specs=(
            pl.BlockSpec((CHUNK, width), lambda k: (k, 0)),
            pl.BlockSpec((2, 256, width), lambda k: (0, 0, 0)),
        ),
        compiler_params=limit,
        cost_estimate=pl.CostEstimate(flops=4 * ROWS * width, bytes_accessed=12 * ROWS * width, transcendentals=0),
    )(scales, params, gradients, columns)
    weights, state, consensus = pl.pallas_call(
        blend_kernel,
        out_shape=(
            jax.ShapeDtypeStruct(params.shape, F32),
            jax.ShapeDtypeStruct((1, RANK, ROWS), F32),
            jax.ShapeDtypeStruct((2,), F32),
        ),
        in_specs=[vmem, vmem, vmem],
        out_specs=(hbm, vmem, smem),
        scratch_shapes=[pltpu.VMEM((ROWS, width), F32), pltpu.SemaphoreType.DMA((CHUNKS,))],
        compiler_params=limit,
    )(back, half, right)
    return weights, jnp.swapaxes(state, 1, 2), consensus, norms


def solution(mesh):
    finer = Mesh(
        mesh.devices.reshape(4, 4, 2, 2, 4), ("gossip_0", "gossip_1", "gossip_2", "mp_0", "mp_1")
    )
    gossip = ("gossip_0", "gossip_1", "gossip_2")
    mp = ("mp_0", "mp_1")
    return jax.shard_map(
        body,
        mesh=finer,
        in_specs=(P(gossip, None, mp), P(gossip, None, None), P(None, gossip, None, mp), P(mp, None), P(None, gossip)),
        out_specs=(P(gossip, None, mp), P(gossip, None, None), P(), P()),
        check_vma=False,
    )
```

```python
import functools

import jax
import jax.numpy as jnp
from jax import lax
from jax.experimental import pallas as pl
from jax.experimental.pallas import tpu as pltpu
from jax.sharding import Mesh
from jax.sharding import PartitionSpec as P

F32 = jnp.float32
BF16 = jnp.bfloat16
HIGHEST = lax.Precision.HIGHEST

NODES = 32
MP = 8
ROWS = 1024
RANK = 64
SLAB = 4096
DEVICES = NODES * MP
QUARTER = ROWS // 4
CHUNKS = 4
CHUNK = ROWS // CHUNKS
PARTS = (("w", 0, 512), ("w", 512, 1024), ("g0", 0, 1024), ("g1", 0, 1024))
MP_ORDER = ("mp_1", "mp_0")
GOSSIP_ORDER = ("gossip_2", "gossip_0", "gossip_1")
ALL_ORDER = ("gossip_2", "mp_1", "mp_0", "gossip_0", "gossip_1")
PLANE = NODES // 2
TOTAL = NODES * ROWS * SLAB

step_size = 1.0
clip_limit = 0.5
mixing = 0.4
epsilon = 1e-06


def lanes(shape):
    return lax.broadcasted_iota(jnp.int32, shape, 1)


def rounded(x):
    return x.astype(BF16).astype(F32)


def split_two(x):
    hi = x.astype(BF16)
    return hi, (x - hi.astype(F32)).astype(BF16)


def dot(a, b, **kw):
    return jnp.dot(a, b, preferred_element_type=F32, **kw)


def project_kernel(part_hbm, w_hbm, g_hbm, c_hbm, p_hbm, out_ref, part, w, g, c, p, gram, stage, sems):
    me = lax.axis_index(GOSSIP_ORDER)
    col = lax.axis_index(MP_ORDER)
    first = pl.multiple_of((col // 2) * QUARTER, QUARTER)
    p_copy = pltpu.make_async_copy(p_hbm, p, sems.at[len(PARTS)])
    p_copy.start()
    loads = []
    for i, (name, begin, end) in enumerate(PARTS):
        rows = pl.ds(begin, end - begin)
        if name == "w":
            copy = pltpu.make_async_copy(w_hbm.at[0, rows], w.at[rows], sems.at[i])
        else:
            r = int(name[1])
            copy = pltpu.make_async_copy(g_hbm.at[r, 0, rows], g.at[r, rows], sems.at[i])
        copy.start()
        loads.append(copy)
    c_copy = pltpu.make_async_copy(c_hbm.at[:, pl.ds(first, QUARTER)], c, sems.at[len(PARTS) + 1])
    c_copy.start()
    part_copy = pltpu.make_async_copy(part_hbm, part, sems.at[len(PARTS) + 2])
    part_copy.start()
    p_copy.wait()
    low = lanes((QUARTER, 128)) < RANK
    pt = p[...]
    hi = rounded(pt)
    lo = rounded(pt - hi)
    right = jnp.concatenate([hi, hi, lo, lo], axis=0).T.astype(BF16)
    gram[...] = lax.dot_general(
        pt, jnp.concatenate([pt, pt], axis=0), (((1,), (1,)), ((), ())),
        precision=HIGHEST, preferred_element_type=F32,
    )
    lane = lanes((1, 128))
    row = jnp.where(lane < RANK, gram[pl.ds(me, 1), :], gram[pl.ds(me + NODES, 1), :])

    def put(j, x):
        stage[pl.ds(j, DEVICES, 8), :] = x

    put(6, jnp.broadcast_to(row, (DEVICES, 128)))
    scalars = jnp.zeros((1, 128), F32)
    for (name, begin, end), copy in zip(PARTS, loads):

        def store(a, value):
            for s in range((end - begin) // 512):
                at = s * 512
                packed = jnp.where(low, value[at : at + 256], value[at + 256 : at + 512])
                put(2 * a + begin // 512 + s, packed)

        copy.wait()
        if name == "w":
            w_hi, w_lo = split_two(w[begin:end, :])
            whole = dot(w_hi, right)
            store(0, whole[:, :128] + whole[:, 128:] + dot(w_lo, right[:, :128]))
        else:
            r = int(name[1])
            grad = g[r]
            whole = dot(grad, right)
            store(1 + r, whole[:, :128] + whole[:, 128:])
            gf = grad.astype(F32)
            squares = jnp.sum((gf * gf).reshape(ROWS // 8, 8, -1), axis=0)
            total = jnp.sum(squares, axis=(0, 1), keepdims=True)
            hi = rounded(total)
            scalars = jnp.where(lane == 64 + 2 * r, hi, scalars)
            scalars = jnp.where(lane == 65 + 2 * r, total - hi, scalars)
    c_copy.wait()
    part_copy.wait()
    for r in range(2):
        mate = part[0, r]
        place = (mate % 2) * PLANE + mate // 2
        scalars = jnp.where(lane == 68 + r, place.astype(F32), scalars)
    ct = c[...].T
    hi = rounded(ct)
    own = jnp.where(col % 2 == 0, hi, ct - hi)
    put(7, jnp.concatenate([own, jnp.zeros_like(own)], axis=1) + scalars)
    out_ref[...] = stage[...].reshape(DEVICES, 8, 128).astype(BF16)


def mix_kernel(in_ref, piece_ref, vec_ref, norm_ref, stage):
    stage[...] = in_ref[...].astype(F32).reshape(DEVICES * 8, 128)

    def got(m, j):
        parts = [stage[pl.ds(8 * PLANE * (core * MP + m) + j, PLANE, 8), :] for core in range(2)]
        return jnp.concatenate(parts, axis=0)

    def summed(j):
        return functools.reduce(lambda x, y: x + y, [got(m, j) for m in range(MP)])

    proj, back0, back1 = [
        jnp.concatenate([summed(2 * a), summed(2 * a + 1)], axis=1) for a in range(3)
    ]
    rows = summed(6)
    extras = [got(m, 7) for m in range(MP)]
    start = jnp.concatenate(
        [extras[2 * k][:, :RANK] + extras[2 * k + 1][:, :RANK] for k in range(4)], axis=1
    )
    scalars = functools.reduce(lambda x, y: x + y, extras)
    lane = lanes((NODES, 128))
    scales = []
    for r in range(2):
        chosen = (lane == 64 + 2 * r) | (lane == 65 + 2 * r)
        total = jnp.sum(jnp.where(chosen, scalars, 0.0), axis=(0, 1), keepdims=True)
        norm = jnp.sqrt(total / TOTAL + epsilon)
        scales.append(step_size * jnp.minimum(1.0, clip_limit / norm))
        norm_ref[r] = norm[0, 0]
    pairing = []
    for r in range(2):
        mate = jnp.sum(jnp.where(lane == 68 + r, extras[0], 0.0), axis=1, keepdims=True)
        column = lanes((NODES, NODES)).astype(F32)
        pairing.append(jnp.where(column == mate, 1.0, 0.0).astype(BF16))

    turned = pltpu.roll(rows, RANK, 1)
    twice = jnp.concatenate(
        [jnp.where(lane < RANK, rows, turned), jnp.where(lane < RANK, turned, rows)], axis=0
    )
    wide = jnp.concatenate([twice, twice], axis=1)
    tall = jnp.concatenate([wide] * 4, axis=0)
    square = (256, 256)
    same = lax.broadcasted_iota(jnp.int32, square, 0) // RANK == lanes(square) // RANK
    gram = jnp.where(same, tall, 0.0)

    def through(x):
        return dot(x, gram, precision=HIGHEST)

    stepped = proj - scales[0] * back0
    coef0 = start - through(start) + stepped
    sent0 = coef0.astype(BF16)
    own0 = sent0.astype(F32)
    drift0 = dot(pairing[0], sent0) - own0
    both = through(jnp.concatenate([drift0, own0], axis=0))
    moved0 = both[:NODES]
    coef1 = own0 - both[NODES:] + (stepped - scales[1] * back1) + mixing * moved0
    sent1 = coef1.astype(BF16)
    own1 = sent1.astype(F32)
    drift1 = dot(pairing[1], sent1) - own1
    moved1 = through(drift1)
    extra = jnp.zeros((NODES, 128), F32)
    for r, (d, moved) in enumerate(((drift0, moved0), (drift1, moved1))):
        total = jnp.sum(d * moved, axis=(0, 1), keepdims=True)
        hi = rounded(total)
        extra = jnp.where(lane == 2 * r, hi, extra)
        extra = jnp.where(lane == 2 * r + 1, total - hi, extra)
    piece = jnp.stack(
        [
            jnp.concatenate([drift0 + drift1, extra], axis=1),
            jnp.concatenate([own1, jnp.zeros((NODES, 128), F32)], axis=1),
        ],
        axis=1,
    ).astype(BF16)
    for core in range(2):
        for m in range(MP):
            piece_ref[core, m] = piece[core * PLANE : (core + 1) * PLANE]
    vec_ref[...] = jnp.concatenate(
        [jnp.broadcast_to(scales[0], (8, 128)), jnp.broadcast_to(scales[1], (8, 128))], axis=0
    )


def step_kernel(vec_ref, w_ref, g_ref, p_ref, out_ref, right_ref):
    scale0 = vec_ref[0:1, 0:1]
    scale1 = vec_ref[8:9, 0:1]
    out_ref[...] = w_ref[0] - scale0 * g_ref[0, 0].astype(F32) - scale1 * g_ref[1, 0].astype(F32)

    @pl.when(pl.program_id(0) == 0)
    def _():
        hi, lo = split_two(p_ref[...])
        right_ref[0] = jnp.concatenate([hi] * 4, axis=0)
        right_ref[1] = jnp.concatenate([lo] * 4, axis=0)


def blend_kernel(in_ref, half_ref, right_ref, out_hbm, pub_ref, cons_ref, out, sems):
    square = (DEVICES, 256)
    block = lanes(square) // RANK
    zero = jnp.zeros(square, BF16)
    copies = []
    for k in range(CHUNKS):
        moved = jnp.where(block == k, in_ref[:, :256], zero)
        drift = dot(moved, right_ref[0]) + dot(moved, right_ref[1])
        at = pl.ds(k * CHUNK, CHUNK)
        out[at, :] = half_ref[at, :] + mixing * drift
        copy = pltpu.make_async_copy(out.at[at], out_hbm.at[0, at], sems.at[k])
        copy.start()
        copies.append(copy)
    pick = (lax.broadcasted_iota(jnp.int32, (256, RANK), 0) % RANK == lanes((256, RANK))).astype(F32)
    pick = pick.astype(BF16)
    for k in range(CHUNKS):
        sent = jnp.where(block == k, in_ref[:, 384:640], zero)
        pub_ref[0, :, k * CHUNK : (k + 1) * CHUNK] = lax.dot_general(
            pick, sent, (((0,), (1,)), ((), ())), preferred_element_type=F32
        )
    extra = in_ref[:, 256:384].astype(F32)
    lane = lanes((DEVICES, 128))
    for r in range(2):
        chosen = (lane == 2 * r) | (lane == 2 * r + 1)
        total = jnp.sum(jnp.where(chosen, extra, 0.0), axis=(0, 1), keepdims=True)
        cons_ref[r] = (total / TOTAL)[0, 0]
    for copy in copies:
        copy.wait()


def body(params, public, gradients, projection, partners):
    width = params.shape[2]
    smem = pl.BlockSpec(memory_space=pltpu.SMEM)
    vmem = pl.BlockSpec(memory_space=pltpu.VMEM)
    hbm = pl.BlockSpec(memory_space=pltpu.HBM)
    limit = pltpu.CompilerParams(vmem_limit_bytes=32 << 20)
    columns = projection.T
    pinned = [
        pltpu.with_memory_space_constraint(x, pltpu.HBM)
        for x in (partners.T, params, gradients, public[0].T, columns)
    ]
    outgoing = pl.pallas_call(
        project_kernel,
        out_shape=jax.ShapeDtypeStruct((DEVICES, 8, 128), BF16),
        in_specs=[hbm] * 5,
        out_specs=vmem,
        scratch_shapes=[
            pltpu.SMEM((1, 2), jnp.int32),
            pltpu.VMEM((ROWS, width), F32),
            pltpu.VMEM((2, ROWS, width), BF16),
            pltpu.VMEM((RANK, QUARTER), F32),
            pltpu.VMEM((RANK, width), F32),
            pltpu.VMEM((RANK, 128), F32),
            pltpu.VMEM((DEVICES * 8, 128), F32),
            pltpu.SemaphoreType.DMA((len(PARTS) + 3,)),
        ],
        compiler_params=limit,
    )(*pinned)
    arrived = lax.all_to_all(outgoing, ALL_ORDER, 0, 0, tiled=True)
    piece, scales, norms = pl.pallas_call(
        mix_kernel,
        out_shape=(
            jax.ShapeDtypeStruct((2, MP, PLANE, 2, 384), BF16),
            jax.ShapeDtypeStruct((16, 128), F32),
            jax.ShapeDtypeStruct((2,), F32),
        ),
        in_specs=[vmem],
        out_specs=(vmem, vmem, smem),
        scratch_shapes=[pltpu.VMEM((DEVICES * 8, 128), F32)],
        compiler_params=limit,
    )(arrived)
    spread = piece.reshape(DEVICES, 2, 384)
    back = lax.all_to_all(spread, ALL_ORDER, 0, 0, tiled=True).reshape(DEVICES, 768)
    half, right = pl.pallas_call(
        step_kernel,
        grid=(CHUNKS,),
        out_shape=(
            jax.ShapeDtypeStruct((ROWS, width), F32),
            jax.ShapeDtypeStruct((2, 256, width), BF16),
        ),
        in_specs=[
            pl.BlockSpec((16, 128), lambda k: (0, 0)),
            pl.BlockSpec((1, CHUNK, width), lambda k: (0, k, 0)),
            pl.BlockSpec((2, 1, CHUNK, width), lambda k: (0, 0, k, 0)),
            pl.BlockSpec((RANK, width), lambda k: (0, 0)),
        ],
        out_specs=(
            pl.BlockSpec((CHUNK, width), lambda k: (k, 0)),
            pl.BlockSpec((2, 256, width), lambda k: (0, 0, 0)),
        ),
        compiler_params=limit,
        cost_estimate=pl.CostEstimate(flops=4 * ROWS * width, bytes_accessed=12 * ROWS * width, transcendentals=0),
    )(scales, pinned[1], pinned[2], columns)
    weights, state, consensus = pl.pallas_call(
        blend_kernel,
        out_shape=(
            jax.ShapeDtypeStruct(params.shape, F32),
            jax.ShapeDtypeStruct((1, RANK, ROWS), F32),
            jax.ShapeDtypeStruct((2,), F32),
        ),
        in_specs=[vmem, vmem, vmem],
        out_specs=(hbm, vmem, smem),
        scratch_shapes=[pltpu.VMEM((ROWS, width), F32), pltpu.SemaphoreType.DMA((CHUNKS,))],
        compiler_params=limit,
    )(back, half, right)
    return weights, jnp.swapaxes(state, 1, 2), consensus, norms


def solution(mesh):
    finer = Mesh(
        mesh.devices.reshape(4, 4, 2, 2, 4), ("gossip_0", "gossip_1", "gossip_2", "mp_0", "mp_1")
    )
    gossip = ("gossip_0", "gossip_1", "gossip_2")
    mp = ("mp_0", "mp_1")
    return jax.shard_map(
        body,
        mesh=finer,
        in_specs=(P(gossip, None, mp), P(gossip, None, None), P(None, gossip, None, mp), P(mp, None), P(None, gossip)),
        out_specs=(P(gossip, None, mp), P(gossip, None, None), P(), P()),
        check_vma=False,
    )
```

```python
import functools

import jax
import jax.numpy as jnp
from jax import lax
from jax.experimental import pallas as pl
from jax.experimental.pallas import tpu as pltpu
from jax.sharding import Mesh
from jax.sharding import PartitionSpec as P

F32 = jnp.float32
BF16 = jnp.bfloat16
HIGHEST = lax.Precision.HIGHEST

NODES = 32
MP = 8
ROWS = 1024
RANK = 64
SLAB = 4096
DEVICES = NODES * MP
QUARTER = ROWS // 4
CHUNKS = 4
CHUNK = ROWS // CHUNKS
PARTS = (("g0", 0, 1024), ("g1", 0, 1024), ("w", 0, 512), ("w", 512, 1024))
MP_ORDER = ("mp_1", "mp_0")
GOSSIP_ORDER = ("gossip_2", "gossip_0", "gossip_1")
ALL_ORDER = ("gossip_2", "mp_1", "mp_0", "gossip_0", "gossip_1")
PLANE = NODES // 2
TOTAL = NODES * ROWS * SLAB

step_size = 1.0
clip_limit = 0.5
mixing = 0.4
epsilon = 1e-06


def lanes(shape):
    return lax.broadcasted_iota(jnp.int32, shape, 1)


def rounded(x):
    return x.astype(BF16).astype(F32)


def split_two(x):
    hi = x.astype(BF16)
    return hi, (x - hi.astype(F32)).astype(BF16)


def dot(a, b, **kw):
    return jnp.dot(a, b, preferred_element_type=F32, **kw)


def project_kernel(part_hbm, w_hbm, g_hbm, c_hbm, p_hbm, out_ref, part, w, g, c, p, stage, sems):
    me = lax.axis_index(GOSSIP_ORDER)
    col = lax.axis_index(MP_ORDER)
    first = pl.multiple_of((col // 2) * QUARTER, QUARTER)
    p_copy = pltpu.make_async_copy(p_hbm, p, sems.at[len(PARTS)])
    p_copy.start()
    loads = []
    for i, (name, begin, end) in enumerate(PARTS):
        rows = pl.ds(begin, end - begin)
        if name == "w":
            copy = pltpu.make_async_copy(w_hbm.at[0, rows], w.at[rows], sems.at[i])
        else:
            r = int(name[1])
            copy = pltpu.make_async_copy(g_hbm.at[r, 0, rows], g.at[r, rows], sems.at[i])
        copy.start()
        loads.append(copy)
    c_copy = pltpu.make_async_copy(c_hbm.at[:, pl.ds(first, QUARTER)], c, sems.at[len(PARTS) + 1])
    c_copy.start()
    part_copy = pltpu.make_async_copy(part_hbm, part, sems.at[len(PARTS) + 2])
    part_copy.start()
    p_copy.wait()
    low = lanes((QUARTER, 128)) < RANK
    pt = p[...]
    hi = rounded(pt)
    lo = rounded(pt - hi)
    right = jnp.concatenate([hi, hi, lo, lo], axis=0).T.astype(BF16)
    pair = jnp.concatenate([p[pl.ds(me, 1), :], p[pl.ds(me + NODES, 1), :], jnp.zeros((14, p.shape[1]), F32)], axis=0)
    pair_hi, pair_lo = split_two(pair)
    lane = lanes((1, 128))

    def put(j, x):
        stage[pl.ds(j, DEVICES, 8), :] = x

    scalars = jnp.zeros((1, 128), F32)
    for (name, begin, end), copy in zip(PARTS, loads):

        def store(a, value):
            for s in range((end - begin) // 512):
                at = s * 512
                packed = jnp.where(low, value[at : at + 256], value[at + 256 : at + 512])
                put(2 * a + begin // 512 + s, packed)

        copy.wait()
        if name == "w":
            w_hi, w_lo = split_two(w[begin:end, :])
            whole = dot(w_hi, right)
            store(0, whole[:, :128] + whole[:, 128:] + dot(w_lo, right[:, :128]))
        else:
            r = int(name[1])
            grad = g[r]
            if r == 0:
                whole = dot(jnp.concatenate([grad, pair_hi, pair_lo], axis=0), right)
                rows = whole[ROWS:, :128] + whole[ROWS:, 128:]
                rows = rows[:16] + rows[16:]
                row = jnp.where(lane < RANK, rows[0:1], rows[1:2])
                put(6, jnp.broadcast_to(row, (DEVICES, 128)))
                whole = whole[:ROWS]
            else:
                whole = dot(grad, right)
            store(1 + r, whole[:, :128] + whole[:, 128:])
            gf = grad.astype(F32)
            squares = jnp.sum((gf * gf).reshape(ROWS // 8, 8, -1), axis=0)
            total = jnp.sum(squares, axis=(0, 1), keepdims=True)
            hi = rounded(total)
            scalars = jnp.where(lane == 64 + 2 * r, hi, scalars)
            scalars = jnp.where(lane == 65 + 2 * r, total - hi, scalars)
    c_copy.wait()
    part_copy.wait()
    for r in range(2):
        mate = part[0, r]
        place = (mate % 2) * PLANE + mate // 2
        scalars = jnp.where(lane == 68 + r, place.astype(F32), scalars)
    ct = c[...].T
    hi = rounded(ct)
    own = jnp.where(col % 2 == 0, hi, ct - hi)
    put(7, jnp.concatenate([own, jnp.zeros_like(own)], axis=1) + scalars)
    out_ref[...] = stage[...].reshape(DEVICES, 8, 128).astype(BF16)


def mix_kernel(in_ref, piece_ref, vec_ref, stage):
    stage[...] = in_ref[...].astype(F32).reshape(DEVICES * 8, 128)

    def got(m, j):
        parts = [stage[pl.ds(8 * PLANE * (core * MP + m) + j, PLANE, 8), :] for core in range(2)]
        return jnp.concatenate(parts, axis=0)

    def summed(j):
        return functools.reduce(lambda x, y: x + y, [got(m, j) for m in range(MP)])

    proj, back0, back1 = [
        jnp.concatenate([summed(2 * a), summed(2 * a + 1)], axis=1) for a in range(3)
    ]
    rows = summed(6)
    extras = [got(m, 7) for m in range(MP)]
    start_hi, start_lo = [
        jnp.concatenate([extras[2 * k + n][:, :RANK] for k in range(4)], axis=1) for n in range(2)
    ]
    scalars = functools.reduce(lambda x, y: x + y, extras)
    lane = lanes((NODES, 128))
    scales, norms = [], []
    for r in range(2):
        chosen = (lane == 64 + 2 * r) | (lane == 65 + 2 * r)
        total = jnp.sum(jnp.where(chosen, scalars, 0.0), axis=(0, 1), keepdims=True)
        norm = jnp.sqrt(total / TOTAL + epsilon)
        scales.append(step_size * jnp.minimum(1.0, clip_limit / norm))
        norms.append(norm)
    pairing = []
    for r in range(2):
        mate = jnp.sum(jnp.where(lane == 68 + r, extras[0], 0.0), axis=1, keepdims=True)
        column = lanes((NODES, NODES)).astype(F32)
        pairing.append(jnp.where(column == mate, 1.0, 0.0).astype(BF16))

    turned = pltpu.roll(rows, RANK, 1)
    twice = jnp.concatenate(
        [jnp.where(lane < RANK, rows, turned), jnp.where(lane < RANK, turned, rows)], axis=0
    )
    wide = jnp.concatenate([twice, twice], axis=1)
    tall = jnp.concatenate([wide] * 4, axis=0)
    square = (256, 256)
    same = lax.broadcasted_iota(jnp.int32, square, 0) // RANK == lanes(square) // RANK
    gram_hi, gram_lo = split_two(jnp.where(same, tall, 0.0))

    def through(pairs):
        upper = jnp.concatenate([x for pair in pairs for x in pair], axis=0)
        lower = jnp.concatenate([pair[0] for pair in pairs], axis=0)
        upper, lower = dot(upper, gram_hi), dot(lower, gram_lo)
        out, at = [], 0
        for n, pair in enumerate(pairs):
            total = lower[n * NODES : (n + 1) * NODES]
            for _ in pair:
                total += upper[at : at + NODES]
                at += NODES
            out.append(total)
        return out

    stepped = proj - scales[0] * back0
    (moved,) = through([(start_hi.astype(BF16), start_lo.astype(BF16))])
    coef0 = start_hi + start_lo - moved + stepped
    sent0 = coef0.astype(BF16)
    own0 = sent0.astype(F32)
    drift0 = dot(pairing[0], sent0) - own0
    moved0, kept0 = through([split_two(drift0), (sent0,)])
    coef1 = own0 - kept0 + (stepped - scales[1] * back1) + mixing * moved0
    sent1 = coef1.astype(BF16)
    own1 = sent1.astype(F32)
    drift1 = dot(pairing[1], sent1) - own1
    (moved1,) = through([split_two(drift1)])
    extra = jnp.zeros((NODES, 128), F32)
    for r, (d, moved) in enumerate(((drift0, moved0), (drift1, moved1))):
        total = jnp.sum(d * moved, axis=(0, 1), keepdims=True)
        hi = rounded(total)
        extra = jnp.where(lane == 2 * r, hi, extra)
        extra = jnp.where(lane == 2 * r + 1, total - hi, extra)
    piece = jnp.stack(
        [
            jnp.concatenate([drift0 + drift1, extra], axis=1),
            jnp.concatenate([own1, jnp.zeros((NODES, 128), F32)], axis=1),
        ],
        axis=1,
    ).astype(BF16)
    for core in range(2):
        for m in range(MP):
            piece_ref[core, m] = piece[core * PLANE : (core + 1) * PLANE]
    vec_ref[...] = jnp.concatenate([jnp.broadcast_to(x, (8, 128)) for x in scales + norms], axis=0)


def step_kernel(vec_ref, w_ref, g_ref, p_ref, out_ref, right_ref, norm_ref):
    scale0 = vec_ref[0:1, 0:1]
    scale1 = vec_ref[8:9, 0:1]
    out_ref[...] = w_ref[0] - scale0 * g_ref[0, 0].astype(F32) - scale1 * g_ref[1, 0].astype(F32)

    @pl.when(pl.program_id(0) == 0)
    def _():
        for r in range(2):
            norm_ref[r] = vec_ref[16 + 8 * r, 0]
        right_ref[...] = jnp.concatenate([p_ref[...].astype(BF16)] * 4, axis=0)


def blend_kernel(in_ref, half_ref, right_ref, out_hbm, pub_hbm, cons_hbm, out, pub, cons, sems):
    square = (DEVICES, 256)
    block = lanes(square) // RANK
    zero = jnp.zeros(square, BF16)
    copies = []

    def send(source, target):
        copy = pltpu.make_async_copy(source, target, sems.at[len(copies)])
        copy.start()
        copies.append(copy)

    def weights(k):
        moved = jnp.where(block == k, in_ref[:, :256], zero)
        drift = dot(moved, right_ref[...])
        for n in range(2):
            begin = n * CHUNK // 2
            at = pl.ds(k * CHUNK + begin, CHUNK // 2)
            out[at, :] = half_ref[at, :] + mixing * drift[begin : begin + CHUNK // 2]
            send(out.at[at], out_hbm.at[0, at])

    weights(0)
    weights(1)
    turned = in_ref[:, 384:640].astype(F32).T
    for k in range(4):
        pub[:, k * QUARTER : (k + 1) * QUARTER] = turned[k * RANK : (k + 1) * RANK, :]
    send(pub, pub_hbm.at[0])
    weights(2)
    extra = jnp.sum(in_ref[:, 256:384].astype(F32), axis=0, keepdims=True)
    lane = lanes((1, 128))
    for r in range(2):
        chosen = (lane == 2 * r) | (lane == 2 * r + 1)
        total = jnp.sum(jnp.where(chosen, extra, 0.0), axis=1, keepdims=True)
        cons[0, r] = (total / TOTAL)[0, 0]
    send(cons, cons_hbm)
    weights(3)
    for copy in copies:
        copy.wait()


def body(params, public, gradients, projection, partners):
    width = params.shape[2]
    smem = pl.BlockSpec(memory_space=pltpu.SMEM)
    vmem = pl.BlockSpec(memory_space=pltpu.VMEM)
    hbm = pl.BlockSpec(memory_space=pltpu.HBM)
    limit = pltpu.CompilerParams(vmem_limit_bytes=32 << 20)
    columns = projection.T
    pinned = [
        pltpu.with_memory_space_constraint(x, pltpu.HBM)
        for x in (partners.T, params, gradients, public[0].T, columns)
    ]
    outgoing = pl.pallas_call(
        project_kernel,
        out_shape=jax.ShapeDtypeStruct((DEVICES, 8, 128), BF16),
        in_specs=[hbm] * 5,
        out_specs=vmem,
        scratch_shapes=[
            pltpu.SMEM((1, 2), jnp.int32),
            pltpu.VMEM((ROWS, width), F32),
            pltpu.VMEM((2, ROWS, width), BF16),
            pltpu.VMEM((RANK, QUARTER), F32),
            pltpu.VMEM((RANK, width), F32),
            pltpu.VMEM((DEVICES * 8, 128), F32),
            pltpu.SemaphoreType.DMA((len(PARTS) + 3,)),
        ],
        compiler_params=limit,
    )(*pinned)
    arrived = lax.all_to_all(outgoing, ALL_ORDER, 0, 0, tiled=True)
    piece, scales = pl.pallas_call(
        mix_kernel,
        out_shape=(
            jax.ShapeDtypeStruct((2, MP, PLANE, 2, 384), BF16),
            jax.ShapeDtypeStruct((32, 128), F32),
        ),
        in_specs=[vmem],
        out_specs=(vmem, vmem),
        scratch_shapes=[pltpu.VMEM((DEVICES * 8, 128), F32)],
        compiler_params=limit,
    )(arrived)
    spread = piece.reshape(DEVICES, 2, 384)
    back = lax.all_to_all(spread, ALL_ORDER, 0, 0, tiled=True).reshape(DEVICES, 768)
    half, right, norms = pl.pallas_call(
        step_kernel,
        grid=(CHUNKS,),
        out_shape=(
            jax.ShapeDtypeStruct((ROWS, width), F32),
            jax.ShapeDtypeStruct((256, width), BF16),
            jax.ShapeDtypeStruct((2,), F32),
        ),
        in_specs=[
            pl.BlockSpec((32, 128), lambda k: (0, 0)),
            pl.BlockSpec((1, CHUNK, width), lambda k: (0, k, 0)),
            pl.BlockSpec((2, 1, CHUNK, width), lambda k: (0, 0, k, 0)),
            pl.BlockSpec((RANK, width), lambda k: (0, 0)),
        ],
        out_specs=(
            pl.BlockSpec((CHUNK, width), lambda k: (k, 0)),
            pl.BlockSpec((256, width), lambda k: (0, 0)),
            smem,
        ),
        compiler_params=limit,
        cost_estimate=pl.CostEstimate(flops=4 * ROWS * width, bytes_accessed=12 * ROWS * width, transcendentals=0),
    )(scales, pinned[1], pinned[2], columns)
    weights, state, consensus = pl.pallas_call(
        blend_kernel,
        out_shape=(
            jax.ShapeDtypeStruct(params.shape, F32),
            jax.ShapeDtypeStruct((1, RANK, ROWS), F32),
            jax.ShapeDtypeStruct((1, 2), F32),
        ),
        in_specs=[vmem, vmem, vmem],
        out_specs=(hbm, hbm, hbm),
        scratch_shapes=[
            pltpu.VMEM((ROWS, width), F32),
            pltpu.VMEM((RANK, ROWS), F32),
            pltpu.SMEM((1, 2), F32),
            pltpu.SemaphoreType.DMA((2 * CHUNKS + 2,)),
        ],
        compiler_params=limit,
    )(back, half, right)
    return weights, jnp.swapaxes(state, 1, 2), consensus[0], norms


def solution(mesh):
    finer = Mesh(
        mesh.devices.reshape(4, 4, 2, 2, 4), ("gossip_0", "gossip_1", "gossip_2", "mp_0", "mp_1")
    )
    gossip = ("gossip_0", "gossip_1", "gossip_2")
    mp = ("mp_0", "mp_1")
    return jax.shard_map(
        body,
        mesh=finer,
        in_specs=(P(gossip, None, mp), P(gossip, None, None), P(None, gossip, None, mp), P(mp, None), P(None, gossip)),
        out_specs=(P(gossip, None, mp), P(gossip, None, None), P(), P()),
        check_vma=False,
    )
```

```python
import functools

import jax
import jax.numpy as jnp
from jax import lax
from jax.experimental import pallas as pl
from jax.experimental.pallas import tpu as pltpu
from jax.sharding import Mesh
from jax.sharding import PartitionSpec as P

F32 = jnp.float32
BF16 = jnp.bfloat16
HIGHEST = lax.Precision.HIGHEST

NODES = 32
MP = 8
ROWS = 1024
RANK = 64
SLAB = 4096
DEVICES = NODES * MP
QUARTER = ROWS // 4
CHUNKS = 4
CHUNK = ROWS // CHUNKS
PARTS = (("g0", 0, 1024), ("g1", 0, 1024), ("w", 0, 512), ("w", 512, 1024))
MP_ORDER = ("mp_1", "mp_0")
GOSSIP_ORDER = ("gossip_2", "gossip_0", "gossip_1")
ALL_ORDER = ("gossip_2", "mp_1", "mp_0", "gossip_0", "gossip_1")
PLANE = NODES // 2
TOTAL = NODES * ROWS * SLAB

step_size = 1.0
clip_limit = 0.5
mixing = 0.4
epsilon = 1e-06


def lanes(shape):
    return lax.broadcasted_iota(jnp.int32, shape, 1)


def rounded(x):
    return x.astype(BF16).astype(F32)


def split_two(x):
    hi = x.astype(BF16)
    return hi, (x - hi.astype(F32)).astype(BF16)


def dot(a, b, **kw):
    return jnp.dot(a, b, preferred_element_type=F32, **kw)


def project_kernel(part_hbm, w_hbm, g_hbm, c_hbm, p_hbm, out_ref, part, w, g, c, p, stage, sems):
    me = lax.axis_index(GOSSIP_ORDER)
    col = lax.axis_index(MP_ORDER)
    first = pl.multiple_of((col // 2) * QUARTER, QUARTER)
    p_copy = pltpu.make_async_copy(p_hbm, p, sems.at[len(PARTS)])
    p_copy.start()
    loads = []
    for i, (name, begin, end) in enumerate(PARTS):
        rows = pl.ds(begin, end - begin)
        if name == "w":
            copy = pltpu.make_async_copy(w_hbm.at[0, rows], w.at[rows], sems.at[i])
        else:
            r = int(name[1])
            copy = pltpu.make_async_copy(g_hbm.at[r, 0, rows], g.at[r, rows], sems.at[i])
        copy.start()
        loads.append(copy)
    c_copy = pltpu.make_async_copy(c_hbm.at[:, pl.ds(first, QUARTER)], c, sems.at[len(PARTS) + 1])
    c_copy.start()
    part_copy = pltpu.make_async_copy(part_hbm, part, sems.at[len(PARTS) + 2])
    part_copy.start()
    p_copy.wait()
    low = lanes((QUARTER, 128)) < RANK
    pt = p[...]
    hi = rounded(pt)
    lo = rounded(pt - hi)
    right = jnp.concatenate([hi, hi, lo, lo], axis=0).T.astype(BF16)
    pair = jnp.concatenate([p[pl.ds(me, 1), :], p[pl.ds(me + NODES, 1), :], jnp.zeros((14, p.shape[1]), F32)], axis=0)
    pair_hi, pair_lo = split_two(pair)
    lane = lanes((1, 128))

    def put(j, x):
        stage[pl.ds(j, DEVICES, 8), :] = x

    scalars = jnp.zeros((1, 128), F32)
    for (name, begin, end), copy in zip(PARTS, loads):

        def store(a, value):
            for s in range((end - begin) // 512):
                at = s * 512
                packed = jnp.where(low, value[at : at + 256], value[at + 256 : at + 512])
                put(2 * a + begin // 512 + s, packed)

        copy.wait()
        if name == "w":
            w_hi, w_lo = split_two(w[begin:end, :])
            whole = dot(w_hi, right)
            store(0, whole[:, :128] + whole[:, 128:] + dot(w_lo, right[:, :128]))
        else:
            r = int(name[1])
            grad = g[r]
            if r == 0:
                whole = dot(jnp.concatenate([grad, pair_hi, pair_lo], axis=0), right)
                rows = whole[ROWS:, :128] + whole[ROWS:, 128:]
                rows = rows[:16] + rows[16:]
                row = jnp.where(lane < RANK, rows[0:1], rows[1:2])
                row = row - jnp.where((lane == me) | (lane == RANK + NODES + me), 1.0 / MP, 0.0)
                put(6, jnp.broadcast_to(row, (DEVICES, 128)))
                whole = whole[:ROWS]
            else:
                whole = dot(grad, right)
            store(1 + r, whole[:, :128] + whole[:, 128:])
            gf = grad.astype(F32)
            squares = jnp.sum((gf * gf).reshape(ROWS // 8, 8, -1), axis=0)
            total = jnp.sum(squares, axis=(0, 1), keepdims=True)
            hi = rounded(total)
            scalars = jnp.where(lane == 64 + 2 * r, hi, scalars)
            scalars = jnp.where(lane == 65 + 2 * r, total - hi, scalars)
    c_copy.wait()
    part_copy.wait()
    for r in range(2):
        mate = part[0, r]
        place = (mate % 2) * PLANE + mate // 2
        scalars = jnp.where(lane == 68 + r, place.astype(F32), scalars)
    ct = c[...].T
    hi = rounded(ct)
    own = jnp.where(col % 2 == 0, hi, ct - hi)
    put(7, jnp.concatenate([own, jnp.zeros_like(own)], axis=1) + scalars)
    out_ref[...] = stage[...].reshape(DEVICES, 8, 128).astype(BF16)


def mix_kernel(in_ref, piece_hbm, vec_ref, stage, piece_ref, sems):
    stage[...] = in_ref[...].astype(F32).reshape(DEVICES * 8, 128)

    def got(m, j):
        parts = [stage[pl.ds(8 * PLANE * (core * MP + m) + j, PLANE, 8), :] for core in range(2)]
        return jnp.concatenate(parts, axis=0)

    def summed(j):
        return functools.reduce(lambda x, y: x + y, [got(m, j) for m in range(MP)])

    proj, back0, back1 = [
        jnp.concatenate([summed(2 * a), summed(2 * a + 1)], axis=1) for a in range(3)
    ]
    rows = summed(6)
    extras = [got(m, 7) for m in range(MP)]
    start_hi, start_lo = [
        jnp.concatenate([extras[2 * k + n][:, :RANK] for k in range(4)], axis=1) for n in range(2)
    ]
    scalars = functools.reduce(lambda x, y: x + y, extras)
    lane = lanes((NODES, 128))
    scales, norms = [], []
    for r in range(2):
        chosen = (lane == 64 + 2 * r) | (lane == 65 + 2 * r)
        total = jnp.sum(jnp.where(chosen, scalars, 0.0), axis=(0, 1), keepdims=True)
        norm = jnp.sqrt(total / TOTAL + epsilon)
        scales.append(step_size * jnp.minimum(1.0, clip_limit / norm))
        norms.append(norm)
    pairing = []
    for r in range(2):
        mate = jnp.sum(jnp.where(lane == 68 + r, extras[0], 0.0), axis=1, keepdims=True)
        column = lanes((NODES, NODES)).astype(F32)
        pairing.append(jnp.where(column == mate, 1.0, 0.0).astype(BF16))

    turned = pltpu.roll(rows, RANK, 1)
    twice = jnp.concatenate(
        [jnp.where(lane < RANK, rows, turned), jnp.where(lane < RANK, turned, rows)], axis=0
    )
    wide = jnp.concatenate([twice, twice], axis=1)
    tall = jnp.concatenate([wide] * 4, axis=0)
    square = (256, 256)
    same = lax.broadcasted_iota(jnp.int32, square, 0) // RANK == lanes(square) // RANK
    gram_hi, gram_lo = split_two(jnp.where(same, tall, 0.0))

    def through(pairs):
        upper = jnp.concatenate([x for pair in pairs for x in pair], axis=0)
        lower = jnp.concatenate([pair[0] for pair in pairs], axis=0)
        upper, lower = dot(upper, gram_hi), dot(lower, gram_lo)
        out, at = [], 0
        for n, pair in enumerate(pairs):
            total = lower[n * NODES : (n + 1) * NODES]
            for _ in pair:
                total += upper[at : at + NODES]
                at += NODES
            out.append(total)
        return out

    stepped = proj - scales[0] * back0
    (moved,) = through([(start_hi.astype(BF16), start_lo.astype(BF16))])
    coef0 = stepped - moved
    sent0 = coef0.astype(BF16)
    own0 = sent0.astype(F32)
    drift0 = dot(pairing[0], sent0) - own0
    moved0, kept0 = through([split_two(drift0), (sent0,)])
    moved0 += drift0
    coef1 = (stepped - scales[1] * back1) - kept0 + mixing * moved0
    sent1 = coef1.astype(BF16)
    own1 = sent1.astype(F32)
    drift1 = dot(pairing[1], sent1) - own1
    (moved1,) = through([split_two(drift1)])
    moved1 += drift1
    extra = jnp.zeros((NODES, 128), F32)
    for r, (d, moved) in enumerate(((drift0, moved0), (drift1, moved1))):
        total = jnp.sum(d * moved, axis=(0, 1), keepdims=True)
        hi = rounded(total)
        extra = jnp.where(lane == 2 * r, hi, extra)
        extra = jnp.where(lane == 2 * r + 1, total - hi, extra)
    piece = jnp.stack(
        [
            jnp.concatenate([drift0 + drift1, extra], axis=1),
            jnp.concatenate([own1, jnp.zeros((NODES, 128), F32)], axis=1),
        ],
        axis=1,
    ).astype(BF16)
    piece_ref[...] = piece.reshape(2, PLANE, 2, 384)
    copies = [pltpu.make_async_copy(piece_ref, piece_hbm.at[:, m], sems.at[m]) for m in range(MP)]
    for copy in copies:
        copy.start()
    vec_ref[...] = jnp.concatenate([jnp.broadcast_to(x, (8, 128)) for x in scales + norms], axis=0)
    for copy in copies:
        copy.wait()


def step_kernel(vec_ref, w_ref, g_ref, p_ref, out_ref, right_ref, norm_ref):
    scale0 = vec_ref[0:1, 0:1]
    scale1 = vec_ref[8:9, 0:1]
    out_ref[...] = w_ref[0] - scale0 * g_ref[0, 0].astype(F32) - scale1 * g_ref[1, 0].astype(F32)

    @pl.when(pl.program_id(0) == 0)
    def _():
        for r in range(2):
            norm_ref[r] = vec_ref[16 + 8 * r, 0]
        right_ref[...] = jnp.concatenate([p_ref[...].astype(BF16)] * 4, axis=0)


def blend_kernel(in_ref, half_ref, right_ref, out_hbm, pub_hbm, cons_hbm, out, pub, cons, sems):
    square = (DEVICES, 256)
    block = lanes(square) // RANK
    zero = jnp.zeros(square, BF16)
    copies = []

    def send(source, target):
        copy = pltpu.make_async_copy(source, target, sems.at[len(copies)])
        copy.start()
        copies.append(copy)

    def weights(k):
        moved = jnp.where(block == k, in_ref[:, :256], zero)
        drift = dot(moved, right_ref[...])
        for n in range(2):
            begin = n * CHUNK // 2
            at = pl.ds(k * CHUNK + begin, CHUNK // 2)
            out[at, :] = half_ref[at, :] + mixing * drift[begin : begin + CHUNK // 2]
            send(out.at[at], out_hbm.at[0, at])

    weights(0)
    weights(1)
    turned = in_ref[:, 384:640].astype(F32).T
    for k in range(4):
        pub[:, k * QUARTER : (k + 1) * QUARTER] = turned[k * RANK : (k + 1) * RANK, :]
    send(pub, pub_hbm.at[0])
    weights(2)
    extra = jnp.sum(in_ref[:, 256:384].astype(F32), axis=0, keepdims=True)
    lane = lanes((1, 128))
    for r in range(2):
        chosen = (lane == 2 * r) | (lane == 2 * r + 1)
        total = jnp.sum(jnp.where(chosen, extra, 0.0), axis=1, keepdims=True)
        cons[0, r] = (total / TOTAL)[0, 0]
    send(cons, cons_hbm)
    weights(3)
    for copy in copies:
        copy.wait()


def body(params, public, gradients, projection, partners):
    width = params.shape[2]
    smem = pl.BlockSpec(memory_space=pltpu.SMEM)
    vmem = pl.BlockSpec(memory_space=pltpu.VMEM)
    hbm = pl.BlockSpec(memory_space=pltpu.HBM)
    limit = pltpu.CompilerParams(vmem_limit_bytes=32 << 20)
    columns = projection.T
    pinned = [
        pltpu.with_memory_space_constraint(x, pltpu.HBM)
        for x in (partners.T, params, gradients, public[0].T, columns)
    ]
    outgoing = pl.pallas_call(
        project_kernel,
        out_shape=jax.ShapeDtypeStruct((DEVICES, 8, 128), BF16),
        in_specs=[hbm] * 5,
        out_specs=vmem,
        scratch_shapes=[
            pltpu.SMEM((1, 2), jnp.int32),
            pltpu.VMEM((ROWS, width), F32),
            pltpu.VMEM((2, ROWS, width), BF16),
            pltpu.VMEM((RANK, QUARTER), F32),
            pltpu.VMEM((RANK, width), F32),
            pltpu.VMEM((DEVICES * 8, 128), F32),
            pltpu.SemaphoreType.DMA((len(PARTS) + 3,)),
        ],
        compiler_params=limit,
    )(*pinned)
    arrived = lax.all_to_all(outgoing, ALL_ORDER, 0, 0, tiled=True)
    piece, scales = pl.pallas_call(
        mix_kernel,
        out_shape=(
            jax.ShapeDtypeStruct((2, MP, PLANE, 2, 384), BF16),
            jax.ShapeDtypeStruct((32, 128), F32),
        ),
        in_specs=[vmem],
        out_specs=(hbm, vmem),
        scratch_shapes=[
            pltpu.VMEM((DEVICES * 8, 128), F32),
            pltpu.VMEM((2, PLANE, 2, 384), BF16),
            pltpu.SemaphoreType.DMA((MP,)),
        ],
        compiler_params=limit,
    )(arrived)
    spread = piece.reshape(DEVICES, 2, 384)
    back = lax.all_to_all(spread, ALL_ORDER, 0, 0, tiled=True).reshape(DEVICES, 768)
    half, right, norms = pl.pallas_call(
        step_kernel,
        grid=(CHUNKS,),
        out_shape=(
            jax.ShapeDtypeStruct((ROWS, width), F32),
            jax.ShapeDtypeStruct((256, width), BF16),
            jax.ShapeDtypeStruct((2,), F32),
        ),
        in_specs=[
            pl.BlockSpec((32, 128), lambda k: (0, 0)),
            pl.BlockSpec((1, CHUNK, width), lambda k: (0, k, 0)),
            pl.BlockSpec((2, 1, CHUNK, width), lambda k: (0, 0, k, 0)),
            pl.BlockSpec((RANK, width), lambda k: (0, 0)),
        ],
        out_specs=(
            pl.BlockSpec((CHUNK, width), lambda k: (k, 0)),
            pl.BlockSpec((256, width), lambda k: (0, 0)),
            smem,
        ),
        compiler_params=limit,
        cost_estimate=pl.CostEstimate(flops=4 * ROWS * width, bytes_accessed=12 * ROWS * width, transcendentals=0),
    )(scales, pinned[1], pinned[2], columns)
    weights, state, consensus = pl.pallas_call(
        blend_kernel,
        out_shape=(
            jax.ShapeDtypeStruct(params.shape, F32),
            jax.ShapeDtypeStruct((1, RANK, ROWS), F32),
            jax.ShapeDtypeStruct((1, 2), F32),
        ),
        in_specs=[vmem, vmem, vmem],
        out_specs=(hbm, hbm, hbm),
        scratch_shapes=[
            pltpu.VMEM((ROWS, width), F32),
            pltpu.VMEM((RANK, ROWS), F32),
            pltpu.SMEM((1, 2), F32),
            pltpu.SemaphoreType.DMA((2 * CHUNKS + 2,)),
        ],
        compiler_params=limit,
    )(back, half, right)
    return weights, jnp.swapaxes(state, 1, 2), consensus[0], norms


def solution(mesh):
    finer = Mesh(
        mesh.devices.reshape(4, 4, 2, 2, 4), ("gossip_0", "gossip_1", "gossip_2", "mp_0", "mp_1")
    )
    gossip = ("gossip_0", "gossip_1", "gossip_2")
    mp = ("mp_0", "mp_1")
    return jax.shard_map(
        body,
        mesh=finer,
        in_specs=(P(gossip, None, mp), P(gossip, None, None), P(None, gossip, None, mp), P(mp, None), P(None, gossip)),
        out_specs=(P(gossip, None, mp), P(gossip, None, None), P(), P()),
        check_vma=False,
    )
```

```python
import jax
import jax.numpy as jnp
from jax import lax
from jax.experimental import pallas as pl
from jax.experimental.pallas import tpu as pltpu
from jax.sharding import Mesh
from jax.sharding import PartitionSpec as P

F32 = jnp.float32
BF16 = jnp.bfloat16
HIGHEST = lax.Precision.HIGHEST

NODES = 32
MP = 8
ROWS = 1024
RANK = 64
SLAB = 4096
DEVICES = NODES * MP
QUARTER = ROWS // 4
CHUNKS = 4
CHUNK = ROWS // CHUNKS
PARTS = (("g0", 0, 1024), ("g1", 0, 1024), ("w", 0, 512), ("w", 512, 1024))
MP_ORDER = ("mp_1", "mp_0")
GOSSIP_ORDER = ("gossip_2", "gossip_0", "gossip_1")
ALL_ORDER = ("gossip_2", "mp_1", "mp_0", "gossip_0", "gossip_1")
PLANE = NODES // 2
TOTAL = NODES * ROWS * SLAB

step_size = 1.0
clip_limit = 0.5
mixing = 0.4
epsilon = 1e-06


def lanes(shape):
    return lax.broadcasted_iota(jnp.int32, shape, 1)


def rounded(x):
    return x.astype(BF16).astype(F32)


def split_two(x):
    hi = x.astype(BF16)
    return hi, (x - hi.astype(F32)).astype(BF16)


def dot(a, b, **kw):
    return jnp.dot(a, b, preferred_element_type=F32, **kw)


def project_kernel(part_hbm, w_hbm, g_hbm, c_hbm, p_hbm, out_ref, part, w, g, c, p, stage, sems):
    me = lax.axis_index(GOSSIP_ORDER)
    col = lax.axis_index(MP_ORDER)
    first = pl.multiple_of((col // 2) * QUARTER, QUARTER)
    p_copy = pltpu.make_async_copy(p_hbm, p, sems.at[len(PARTS)])
    p_copy.start()
    loads = []
    for i, (name, begin, end) in enumerate(PARTS):
        rows = pl.ds(begin, end - begin)
        if name == "w":
            copy = pltpu.make_async_copy(w_hbm.at[0, rows], w.at[rows], sems.at[i])
        else:
            r = int(name[1])
            copy = pltpu.make_async_copy(g_hbm.at[r, 0, rows], g.at[r, rows], sems.at[i])
        copy.start()
        loads.append(copy)
    c_copy = pltpu.make_async_copy(c_hbm.at[:, pl.ds(first, QUARTER)], c, sems.at[len(PARTS) + 1])
    c_copy.start()
    part_copy = pltpu.make_async_copy(part_hbm, part, sems.at[len(PARTS) + 2])
    part_copy.start()
    p_copy.wait()
    low = lanes((QUARTER, 128)) < RANK
    pt = p[...]
    hi = rounded(pt)
    lo = rounded(pt - hi)
    right = jnp.concatenate([hi, hi, lo, lo], axis=0).T.astype(BF16)
    pair = jnp.concatenate([p[pl.ds(me, 1), :], p[pl.ds(me + NODES, 1), :], jnp.zeros((14, p.shape[1]), F32)], axis=0)
    pair_hi, pair_lo = split_two(pair)
    lane = lanes((1, 128))

    def put(j, x):
        stage[pl.ds(j, DEVICES, 8), :] = x

    scalars = jnp.zeros((1, 128), F32)
    for (name, begin, end), copy in zip(PARTS, loads):

        def store(a, value):
            for s in range((end - begin) // 512):
                at = s * 512
                packed = jnp.where(low, value[at : at + 256], value[at + 256 : at + 512])
                put(2 * a + begin // 512 + s, packed)

        copy.wait()
        if name == "w":
            w_hi, w_lo = split_two(w[begin:end, :])
            whole = dot(w_hi, right)
            store(0, whole[:, :128] + whole[:, 128:] + dot(w_lo, right[:, :128]))
        else:
            r = int(name[1])
            grad = g[r]
            if r == 0:
                whole = dot(jnp.concatenate([grad, pair_hi, pair_lo], axis=0), right)
                rows = whole[ROWS:, :128] + whole[ROWS:, 128:]
                rows = rows[:16] + rows[16:]
                row = jnp.where(lane < RANK, rows[0:1], rows[1:2])
                row = row - jnp.where((lane == me) | (lane == RANK + NODES + me), 1.0 / MP, 0.0)
                put(6, jnp.broadcast_to(row, (DEVICES, 128)))
                whole = whole[:ROWS]
            else:
                whole = dot(grad, right)
            store(1 + r, whole[:, :128] + whole[:, 128:])
            gf = grad.astype(F32)
            squares = jnp.sum((gf * gf).reshape(ROWS // 8, 8, -1), axis=0)
            total = jnp.sum(squares, axis=(0, 1), keepdims=True)
            hi = rounded(total)
            scalars = jnp.where(lane == 64 + 2 * r, hi, scalars)
            scalars = jnp.where(lane == 65 + 2 * r, total - hi, scalars)
    c_copy.wait()
    part_copy.wait()
    for r in range(2):
        mate = part[0, r]
        place = (mate % 2) * PLANE + mate // 2
        scalars = jnp.where(lane == 68 + r, place.astype(F32), scalars)
    ct = c[...].T
    hi = rounded(ct)
    own = jnp.where(col % 2 == 0, hi, ct - hi)
    put(7, jnp.concatenate([own, jnp.zeros_like(own)], axis=1) + scalars)
    out_ref[...] = stage[...].reshape(DEVICES, 8, 128).astype(BF16)


def mix_kernel(in_ref, piece_hbm, vec_ref, stage, sums, piece_ref, sems):
    value = in_ref[...].astype(F32)
    stage[...] = value.reshape(DEVICES * 8, 128)
    value = jnp.sum(value.reshape(2, MP, PLANE, 8, 128), axis=1)
    sums[...] = value.reshape(NODES * 8, 128)

    def got(m, j):
        parts = [stage[pl.ds(8 * PLANE * (core * MP + m) + j, PLANE, 8), :] for core in range(2)]
        return jnp.concatenate(parts, axis=0)

    def summed(j):
        return sums[pl.ds(j, NODES, 8), :]

    proj, back0, back1 = [
        jnp.concatenate([summed(2 * a), summed(2 * a + 1)], axis=1) for a in range(3)
    ]
    rows = summed(6)
    extras = [got(m, 7) for m in range(MP)]
    start_hi, start_lo = [
        jnp.concatenate([extras[2 * k + n][:, :RANK] for k in range(4)], axis=1) for n in range(2)
    ]
    scalars = summed(7)
    lane = lanes((NODES, 128))
    scales, norms = [], []
    for r in range(2):
        chosen = (lane == 64 + 2 * r) | (lane == 65 + 2 * r)
        total = jnp.sum(jnp.where(chosen, scalars, 0.0), axis=(0, 1), keepdims=True)
        norm = jnp.sqrt(total / TOTAL + epsilon)
        scales.append(step_size * jnp.minimum(1.0, clip_limit / norm))
        norms.append(norm)
    pairing = []
    for r in range(2):
        mate = jnp.sum(jnp.where(lane == 68 + r, extras[0], 0.0), axis=1, keepdims=True)
        column = lanes((NODES, NODES)).astype(F32)
        pairing.append(jnp.where(column == mate, 1.0, 0.0).astype(BF16))

    turned = pltpu.roll(rows, RANK, 1)
    twice = jnp.concatenate(
        [jnp.where(lane < RANK, rows, turned), jnp.where(lane < RANK, turned, rows)], axis=0
    )
    wide = jnp.concatenate([twice, twice], axis=1)
    tall = jnp.concatenate([wide] * 4, axis=0)
    square = (256, 256)
    same = lax.broadcasted_iota(jnp.int32, square, 0) // RANK == lanes(square) // RANK
    gram_hi, gram_lo = split_two(jnp.where(same, tall, 0.0))

    def through(pairs):
        upper = jnp.concatenate([x for pair in pairs for x in pair], axis=0)
        lower = jnp.concatenate([pair[0] for pair in pairs], axis=0)
        upper, lower = dot(upper, gram_hi), dot(lower, gram_lo)
        out, at = [], 0
        for n, pair in enumerate(pairs):
            total = lower[n * NODES : (n + 1) * NODES]
            for _ in pair:
                total += upper[at : at + NODES]
                at += NODES
            out.append(total)
        return out

    stepped = proj - scales[0] * back0
    (moved,) = through([(start_hi.astype(BF16), start_lo.astype(BF16))])
    coef0 = stepped - moved
    sent0 = coef0.astype(BF16)
    own0 = sent0.astype(F32)
    drift0 = dot(pairing[0], sent0) - own0
    moved0, kept0 = through([split_two(drift0), (sent0,)])
    moved0 += drift0
    coef1 = (stepped - scales[1] * back1) - kept0 + mixing * moved0
    sent1 = coef1.astype(BF16)
    own1 = sent1.astype(F32)
    drift1 = dot(pairing[1], sent1) - own1
    (moved1,) = through([split_two(drift1)])
    moved1 += drift1
    extra = jnp.zeros((NODES, 128), F32)
    for r, (d, moved) in enumerate(((drift0, moved0), (drift1, moved1))):
        total = jnp.sum(d * moved, axis=(0, 1), keepdims=True)
        hi = rounded(total)
        extra = jnp.where(lane == 2 * r, hi, extra)
        extra = jnp.where(lane == 2 * r + 1, total - hi, extra)
    piece = jnp.stack(
        [
            jnp.concatenate([drift0 + drift1, extra], axis=1),
            jnp.concatenate([own1, jnp.zeros((NODES, 128), F32)], axis=1),
        ],
        axis=1,
    ).astype(BF16)
    piece_ref[...] = piece.reshape(2, PLANE, 2, 384)
    copies = [pltpu.make_async_copy(piece_ref, piece_hbm.at[:, m], sems.at[m]) for m in range(MP)]
    for copy in copies:
        copy.start()
    vec_ref[...] = jnp.concatenate([jnp.broadcast_to(x, (8, 128)) for x in scales + norms], axis=0)
    for copy in copies:
        copy.wait()


def step_kernel(vec_ref, w_ref, g_ref, p_ref, out_ref, right_ref, norm_ref):
    scale0 = vec_ref[0:1, 0:1]
    scale1 = vec_ref[8:9, 0:1]
    out_ref[...] = w_ref[0] - scale0 * g_ref[0, 0].astype(F32) - scale1 * g_ref[1, 0].astype(F32)

    @pl.when(pl.program_id(0) == 0)
    def _():
        for r in range(2):
            norm_ref[r] = vec_ref[16 + 8 * r, 0]
        right_ref[...] = jnp.concatenate([p_ref[...].astype(BF16)] * 4, axis=0)


def blend_kernel(in_ref, half_ref, right_ref, out_hbm, pub_hbm, cons_hbm, out, pub, cons, sems):
    square = (DEVICES, 256)
    block = lanes(square) // RANK
    zero = jnp.zeros(square, BF16)
    copies = []

    def send(source, target):
        copy = pltpu.make_async_copy(source, target, sems.at[len(copies)])
        copy.start()
        copies.append(copy)

    def weights(k):
        moved = jnp.where(block == k, in_ref[:, :256], zero)
        drift = dot(moved, right_ref[...])
        for n in range(2):
            begin = n * CHUNK // 2
            at = pl.ds(k * CHUNK + begin, CHUNK // 2)
            out[at, :] = half_ref[at, :] + mixing * drift[begin : begin + CHUNK // 2]
            send(out.at[at], out_hbm.at[0, at])

    weights(0)
    weights(1)
    turned = in_ref[:, 384:640].astype(F32).T
    for k in range(4):
        pub[:, k * QUARTER : (k + 1) * QUARTER] = turned[k * RANK : (k + 1) * RANK, :]
    send(pub, pub_hbm.at[0])
    weights(2)
    extra = jnp.sum(in_ref[:, 256:384].astype(F32), axis=0, keepdims=True)
    lane = lanes((1, 128))
    for r in range(2):
        chosen = (lane == 2 * r) | (lane == 2 * r + 1)
        total = jnp.sum(jnp.where(chosen, extra, 0.0), axis=1, keepdims=True)
        cons[0, r] = (total / TOTAL)[0, 0]
    send(cons, cons_hbm)
    weights(3)
    for copy in copies:
        copy.wait()


def body(params, public, gradients, projection, partners):
    width = params.shape[2]
    smem = pl.BlockSpec(memory_space=pltpu.SMEM)
    vmem = pl.BlockSpec(memory_space=pltpu.VMEM)
    hbm = pl.BlockSpec(memory_space=pltpu.HBM)
    limit = pltpu.CompilerParams(vmem_limit_bytes=32 << 20)
    columns = projection.T
    pinned = [
        pltpu.with_memory_space_constraint(x, pltpu.HBM)
        for x in (partners.T, params, gradients, public[0].T, columns)
    ]
    outgoing = pl.pallas_call(
        project_kernel,
        out_shape=jax.ShapeDtypeStruct((DEVICES, 8, 128), BF16),
        in_specs=[hbm] * 5,
        out_specs=vmem,
        scratch_shapes=[
            pltpu.SMEM((1, 2), jnp.int32),
            pltpu.VMEM((ROWS, width), F32),
            pltpu.VMEM((2, ROWS, width), BF16),
            pltpu.VMEM((RANK, QUARTER), F32),
            pltpu.VMEM((RANK, width), F32),
            pltpu.VMEM((DEVICES * 8, 128), F32),
            pltpu.SemaphoreType.DMA((len(PARTS) + 3,)),
        ],
        compiler_params=limit,
    )(*pinned)
    arrived = lax.all_to_all(outgoing, ALL_ORDER, 0, 0, tiled=True)
    piece, scales = pl.pallas_call(
        mix_kernel,
        out_shape=(
            jax.ShapeDtypeStruct((2, MP, PLANE, 2, 384), BF16),
            jax.ShapeDtypeStruct((32, 128), F32),
        ),
        in_specs=[vmem],
        out_specs=(hbm, vmem),
        scratch_shapes=[
            pltpu.VMEM((DEVICES * 8, 128), F32),
            pltpu.VMEM((NODES * 8, 128), F32),
            pltpu.VMEM((2, PLANE, 2, 384), BF16),
            pltpu.SemaphoreType.DMA((MP,)),
        ],
        compiler_params=limit,
    )(arrived)
    spread = piece.reshape(DEVICES, 2, 384)
    back = lax.all_to_all(spread, ALL_ORDER, 0, 0, tiled=True).reshape(DEVICES, 768)
    half, right, norms = pl.pallas_call(
        step_kernel,
        grid=(CHUNKS,),
        out_shape=(
            jax.ShapeDtypeStruct((ROWS, width), F32),
            jax.ShapeDtypeStruct((256, width), BF16),
            jax.ShapeDtypeStruct((2,), F32),
        ),
        in_specs=[
            pl.BlockSpec((32, 128), lambda k: (0, 0)),
            pl.BlockSpec((1, CHUNK, width), lambda k: (0, k, 0)),
            pl.BlockSpec((2, 1, CHUNK, width), lambda k: (0, 0, k, 0)),
            pl.BlockSpec((RANK, width), lambda k: (0, 0)),
        ],
        out_specs=(
            pl.BlockSpec((CHUNK, width), lambda k: (k, 0)),
            pl.BlockSpec((256, width), lambda k: (0, 0)),
            smem,
        ),
        compiler_params=limit,
        cost_estimate=pl.CostEstimate(flops=4 * ROWS * width, bytes_accessed=12 * ROWS * width, transcendentals=0),
    )(scales, pinned[1], pinned[2], columns)
    weights, state, consensus = pl.pallas_call(
        blend_kernel,
        out_shape=(
            jax.ShapeDtypeStruct(params.shape, F32),
            jax.ShapeDtypeStruct((1, RANK, ROWS), F32),
            jax.ShapeDtypeStruct((1, 2), F32),
        ),
        in_specs=[vmem, vmem, vmem],
        out_specs=(hbm, hbm, hbm),
        scratch_shapes=[
            pltpu.VMEM((ROWS, width), F32),
            pltpu.VMEM((RANK, ROWS), F32),
            pltpu.SMEM((1, 2), F32),
            pltpu.SemaphoreType.DMA((2 * CHUNKS + 2,)),
        ],
        compiler_params=limit,
    )(back, half, right)
    return weights, jnp.swapaxes(state, 1, 2), consensus[0], norms


def solution(mesh):
    finer = Mesh(
        mesh.devices.reshape(4, 4, 2, 2, 4), ("gossip_0", "gossip_1", "gossip_2", "mp_0", "mp_1")
    )
    gossip = ("gossip_0", "gossip_1", "gossip_2")
    mp = ("mp_0", "mp_1")
    return jax.shard_map(
        body,
        mesh=finer,
        in_specs=(P(gossip, None, mp), P(gossip, None, None), P(None, gossip, None, mp), P(mp, None), P(None, gossip)),
        out_specs=(P(gossip, None, mp), P(gossip, None, None), P(), P()),
        check_vma=False,
    )
```

```python
import jax
import jax.numpy as jnp
from jax import lax
from jax.experimental import pallas as pl
from jax.experimental.pallas import tpu as pltpu
from jax.sharding import Mesh
from jax.sharding import PartitionSpec as P

F32 = jnp.float32
BF16 = jnp.bfloat16
HIGHEST = lax.Precision.HIGHEST

NODES = 32
MP = 8
ROWS = 1024
RANK = 64
SLAB = 4096
DEVICES = NODES * MP
QUARTER = ROWS // 4
CHUNKS = 4
CHUNK = ROWS // CHUNKS
PARTS = (("g0", 0, 1024), ("g1", 0, 1024), ("w", 0, 512), ("w", 512, 1024))
MP_ORDER = ("mp_1", "mp_0")
GOSSIP_ORDER = ("gossip_2", "gossip_0", "gossip_1")
ALL_ORDER = ("gossip_2", "mp_1", "mp_0", "gossip_0", "gossip_1")
PLANE = NODES // 2
TOTAL = NODES * ROWS * SLAB

step_size = 1.0
clip_limit = 0.5
mixing = 0.4
epsilon = 1e-06


def lanes(shape):
    return lax.broadcasted_iota(jnp.int32, shape, 1)


def rounded(x):
    return x.astype(BF16).astype(F32)


def split_two(x):
    hi = x.astype(BF16)
    return hi, (x - hi.astype(F32)).astype(BF16)


def dot(a, b, **kw):
    return jnp.dot(a, b, preferred_element_type=F32, **kw)


def project_kernel(part_hbm, w_hbm, g_hbm, c_hbm, p_hbm, out_ref, part, w, g, c, p, stage, sems):
    me = lax.axis_index(GOSSIP_ORDER)
    col = lax.axis_index(MP_ORDER)
    first = pl.multiple_of((col // 2) * QUARTER, QUARTER)
    p_copy = pltpu.make_async_copy(p_hbm, p, sems.at[len(PARTS)])
    p_copy.start()
    loads = []
    for i, (name, begin, end) in enumerate(PARTS):
        rows = pl.ds(begin, end - begin)
        if name == "w":
            copy = pltpu.make_async_copy(w_hbm.at[0, rows], w.at[rows], sems.at[i])
        else:
            r = int(name[1])
            copy = pltpu.make_async_copy(g_hbm.at[r, 0, rows], g.at[r, rows], sems.at[i])
        copy.start()
        loads.append(copy)
    c_copy = pltpu.make_async_copy(c_hbm.at[:, pl.ds(first, QUARTER)], c, sems.at[len(PARTS) + 1])
    c_copy.start()
    part_copy = pltpu.make_async_copy(part_hbm, part, sems.at[len(PARTS) + 2])
    part_copy.start()
    p_copy.wait()
    low = lanes((QUARTER, 128)) < RANK
    pt = p[...]
    hi = rounded(pt)
    lo = rounded(pt - hi)
    right = jnp.concatenate([hi, hi, lo, lo], axis=0).T.astype(BF16)
    pair = jnp.concatenate([p[pl.ds(me, 1), :], p[pl.ds(me + NODES, 1), :], jnp.zeros((14, p.shape[1]), F32)], axis=0)
    pair_hi, pair_lo = split_two(pair)
    lane = lanes((1, 128))

    def put(j, x):
        stage[pl.ds(j, DEVICES, 8), :] = x

    scalars = jnp.zeros((1, 128), F32)
    for (name, begin, end), copy in zip(PARTS, loads):

        def store(a, value):
            for s in range((end - begin) // 512):
                at = s * 512
                packed = jnp.where(low, value[at : at + 256], value[at + 256 : at + 512])
                put(2 * a + begin // 512 + s, packed)

        copy.wait()
        if name == "w":
            w_hi, w_lo = split_two(w[begin:end, :])
            whole = dot(w_hi, right)
            store(0, whole[:, :128] + whole[:, 128:] + dot(w_lo, right[:, :128]))
        else:
            r = int(name[1])
            grad = g[r]
            if r == 0:
                whole = dot(jnp.concatenate([grad, pair_hi, pair_lo], axis=0), right)
                rows = whole[ROWS:, :128] + whole[ROWS:, 128:]
                rows = rows[:16] + rows[16:]
                row = jnp.where(lane < RANK, rows[0:1], rows[1:2])
                row = row - jnp.where((lane == me) | (lane == RANK + NODES + me), 1.0 / MP, 0.0)
                put(6, jnp.broadcast_to(row, (DEVICES, 128)))
                whole = whole[:ROWS]
            else:
                whole = dot(grad, right)
            store(1 + r, whole[:, :128] + whole[:, 128:])
            gf = grad.astype(F32)
            squares = jnp.sum((gf * gf).reshape(ROWS // 8, 8, -1), axis=0)
            total = jnp.sum(squares, axis=(0, 1), keepdims=True)
            hi = rounded(total)
            scalars = jnp.where(lane == 64 + 2 * r, hi, scalars)
            scalars = jnp.where(lane == 65 + 2 * r, total - hi, scalars)
    c_copy.wait()
    part_copy.wait()
    for r in range(2):
        mate = part[0, r]
        place = (mate % 2) * PLANE + mate // 2
        scalars = jnp.where(lane == 68 + r, place.astype(F32), scalars)
    ct = c[...].T
    hi = rounded(ct)
    own = jnp.where(col % 2 == 0, hi, ct - hi)
    put(7, jnp.concatenate([own, jnp.zeros_like(own)], axis=1) + scalars)
    out_ref[...] = stage[...].reshape(DEVICES, 8, 128).astype(BF16)


def mix_kernel(in_ref, piece_hbm, vec_ref, stage, sums, piece_ref, sems):
    value = in_ref[...].astype(F32)
    stage[...] = value.reshape(DEVICES * 8, 128)
    value = jnp.sum(value.reshape(2, MP, PLANE, 8, 128), axis=1)
    sums[...] = value.reshape(NODES * 8, 128)

    def got(m, j):
        parts = [stage[pl.ds(8 * PLANE * (core * MP + m) + j, PLANE, 8), :] for core in range(2)]
        return jnp.concatenate(parts, axis=0)

    def summed(j):
        return sums[pl.ds(j, NODES, 8), :]

    proj, back0, back1 = [
        jnp.concatenate([summed(2 * a), summed(2 * a + 1)], axis=1) for a in range(3)
    ]
    rows = summed(6)
    extras = [got(m, 7) for m in range(MP)]
    start_hi, start_lo = [
        jnp.concatenate([extras[2 * k + n][:, :RANK] for k in range(4)], axis=1) for n in range(2)
    ]
    scalars = summed(7)
    lane = lanes((NODES, 128))
    scales, norms = [], []
    for r in range(2):
        chosen = (lane == 64 + 2 * r) | (lane == 65 + 2 * r)
        total = jnp.sum(jnp.where(chosen, scalars, 0.0), axis=(0, 1), keepdims=True)
        norm = jnp.sqrt(total / TOTAL + epsilon)
        scales.append(step_size * jnp.minimum(1.0, clip_limit / norm))
        norms.append(norm)
    pairing = []
    for r in range(2):
        mate = jnp.sum(jnp.where(lane == 68 + r, extras[0], 0.0), axis=1, keepdims=True)
        column = lanes((NODES, NODES)).astype(F32)
        pairing.append(jnp.where(column == mate, 1.0, 0.0).astype(BF16))

    turned = pltpu.roll(rows, RANK, 1)
    twice = jnp.concatenate(
        [jnp.where(lane < RANK, rows, turned), jnp.where(lane < RANK, turned, rows)], axis=0
    )
    wide = jnp.concatenate([twice, twice], axis=1)
    tall = jnp.concatenate([wide] * 4, axis=0)
    square = (256, 256)
    same = lax.broadcasted_iota(jnp.int32, square, 0) // RANK == lanes(square) // RANK
    gram_hi, gram_lo = split_two(jnp.where(same, tall, 0.0))

    def through(pairs):
        upper = jnp.concatenate([x for pair in pairs for x in pair], axis=0)
        lower = jnp.concatenate([pair[0] for pair in pairs], axis=0)
        upper, lower = dot(upper, gram_hi), dot(lower, gram_lo)
        out, at = [], 0
        for n, pair in enumerate(pairs):
            total = lower[n * NODES : (n + 1) * NODES]
            for _ in pair:
                total += upper[at : at + NODES]
                at += NODES
            out.append(total)
        return out

    stepped = proj - scales[0] * back0
    (moved,) = through([(start_hi.astype(BF16), start_lo.astype(BF16))])
    coef0 = stepped - moved
    sent0 = coef0.astype(BF16)
    own0 = sent0.astype(F32)
    drift0 = dot(pairing[0], sent0) - own0
    moved0, kept0 = through([split_two(drift0), (sent0,)])
    moved0 += drift0
    coef1 = (stepped - scales[1] * back1) - kept0 + mixing * moved0
    sent1 = coef1.astype(BF16)
    own1 = sent1.astype(F32)
    drift1 = dot(pairing[1], sent1) - own1
    copies = []

    def send(begin, width, upper, lower):
        part = jnp.stack([upper, lower], axis=1).astype(BF16).reshape(2, PLANE, 2, width)
        piece_ref[:, :, :, begin : begin + width] = part
        at = pl.ds(begin, width)
        for m in range(MP):
            copy = pltpu.make_async_copy(
                piece_ref.at[:, :, :, at], piece_hbm.at[:, m, :, :, at], sems.at[len(copies)]
            )
            copy.start()
            copies.append(copy)

    send(0, 256, drift0 + drift1, own1)
    (moved1,) = through([split_two(drift1)])
    moved1 += drift1
    extra = jnp.zeros((NODES, 128), F32)
    for r, (d, moved) in enumerate(((drift0, moved0), (drift1, moved1))):
        total = jnp.sum(d * moved, axis=(0, 1), keepdims=True)
        hi = rounded(total)
        extra = jnp.where(lane == 2 * r, hi, extra)
        extra = jnp.where(lane == 2 * r + 1, total - hi, extra)
    send(256, 128, extra, jnp.zeros((NODES, 128), F32))
    vec_ref[...] = jnp.concatenate([jnp.broadcast_to(x, (8, 128)) for x in scales + norms], axis=0)
    for copy in copies:
        copy.wait()


def step_kernel(vec_ref, w_ref, g_ref, p_ref, out_ref, right_ref, norm_ref):
    scale0 = vec_ref[0:1, 0:1]
    scale1 = vec_ref[8:9, 0:1]
    out_ref[...] = w_ref[0] - scale0 * g_ref[0, 0].astype(F32) - scale1 * g_ref[1, 0].astype(F32)

    @pl.when(pl.program_id(0) == 0)
    def _():
        for r in range(2):
            norm_ref[r] = vec_ref[16 + 8 * r, 0]
        right_ref[...] = jnp.concatenate([p_ref[...].astype(BF16)] * 4, axis=0)


def blend_kernel(in_ref, half_ref, right_ref, out_hbm, pub_hbm, cons_hbm, out, pub, cons, sems):
    square = (DEVICES, 256)
    block = lanes(square) // RANK
    zero = jnp.zeros(square, BF16)
    copies = []

    def send(source, target):
        copy = pltpu.make_async_copy(source, target, sems.at[len(copies)])
        copy.start()
        copies.append(copy)

    def weights(k):
        moved = jnp.where(block == k, in_ref[:, :256], zero)
        drift = dot(moved, right_ref[...])
        for n in range(2):
            begin = n * CHUNK // 2
            at = pl.ds(k * CHUNK + begin, CHUNK // 2)
            out[at, :] = half_ref[at, :] + mixing * drift[begin : begin + CHUNK // 2]
            send(out.at[at], out_hbm.at[0, at])

    weights(0)
    weights(1)
    turned = in_ref[:, 384:640].astype(F32).T
    for k in range(4):
        pub[:, k * QUARTER : (k + 1) * QUARTER] = turned[k * RANK : (k + 1) * RANK, :]
    send(pub, pub_hbm.at[0])
    weights(2)
    extra = jnp.sum(in_ref[:, 256:384].astype(F32), axis=0, keepdims=True)
    lane = lanes((1, 128))
    for r in range(2):
        chosen = (lane == 2 * r) | (lane == 2 * r + 1)
        total = jnp.sum(jnp.where(chosen, extra, 0.0), axis=1, keepdims=True)
        cons[0, r] = (total / TOTAL)[0, 0]
    send(cons, cons_hbm)
    weights(3)
    for copy in copies:
        copy.wait()


def body(params, public, gradients, projection, partners):
    width = params.shape[2]
    smem = pl.BlockSpec(memory_space=pltpu.SMEM)
    vmem = pl.BlockSpec(memory_space=pltpu.VMEM)
    hbm = pl.BlockSpec(memory_space=pltpu.HBM)
    limit = pltpu.CompilerParams(vmem_limit_bytes=32 << 20)
    columns = projection.T
    pinned = [
        pltpu.with_memory_space_constraint(x, pltpu.HBM)
        for x in (partners.T, params, gradients, public[0].T, columns)
    ]
    outgoing = pl.pallas_call(
        project_kernel,
        out_shape=jax.ShapeDtypeStruct((DEVICES, 8, 128), BF16),
        in_specs=[hbm] * 5,
        out_specs=vmem,
        scratch_shapes=[
            pltpu.SMEM((1, 2), jnp.int32),
            pltpu.VMEM((ROWS, width), F32),
            pltpu.VMEM((2, ROWS, width), BF16),
            pltpu.VMEM((RANK, QUARTER), F32),
            pltpu.VMEM((RANK, width), F32),
            pltpu.VMEM((DEVICES * 8, 128), F32),
            pltpu.SemaphoreType.DMA((len(PARTS) + 3,)),
        ],
        compiler_params=limit,
    )(*pinned)
    arrived = lax.all_to_all(outgoing, ALL_ORDER, 0, 0, tiled=True)
    piece, scales = pl.pallas_call(
        mix_kernel,
        out_shape=(
            jax.ShapeDtypeStruct((2, MP, PLANE, 2, 384), BF16),
            jax.ShapeDtypeStruct((32, 128), F32),
        ),
        in_specs=[vmem],
        out_specs=(hbm, vmem),
        scratch_shapes=[
            pltpu.VMEM((DEVICES * 8, 128), F32),
            pltpu.VMEM((NODES * 8, 128), F32),
            pltpu.VMEM((2, PLANE, 2, 384), BF16),
            pltpu.SemaphoreType.DMA((2 * MP,)),
        ],
        compiler_params=limit,
    )(arrived)
    spread = piece.reshape(DEVICES, 2, 384)
    back = lax.all_to_all(spread, ALL_ORDER, 0, 0, tiled=True).reshape(DEVICES, 768)
    half, right, norms = pl.pallas_call(
        step_kernel,
        grid=(CHUNKS,),
        out_shape=(
            jax.ShapeDtypeStruct((ROWS, width), F32),
            jax.ShapeDtypeStruct((256, width), BF16),
            jax.ShapeDtypeStruct((2,), F32),
        ),
        in_specs=[
            pl.BlockSpec((32, 128), lambda k: (0, 0)),
            pl.BlockSpec((1, CHUNK, width), lambda k: (0, k, 0)),
            pl.BlockSpec((2, 1, CHUNK, width), lambda k: (0, 0, k, 0)),
            pl.BlockSpec((RANK, width), lambda k: (0, 0)),
        ],
        out_specs=(
            pl.BlockSpec((CHUNK, width), lambda k: (k, 0)),
            pl.BlockSpec((256, width), lambda k: (0, 0)),
            smem,
        ),
        compiler_params=limit,
        cost_estimate=pl.CostEstimate(flops=4 * ROWS * width, bytes_accessed=12 * ROWS * width, transcendentals=0),
    )(scales, pinned[1], pinned[2], columns)
    weights, state, consensus = pl.pallas_call(
        blend_kernel,
        out_shape=(
            jax.ShapeDtypeStruct(params.shape, F32),
            jax.ShapeDtypeStruct((1, RANK, ROWS), F32),
            jax.ShapeDtypeStruct((1, 2), F32),
        ),
        in_specs=[vmem, vmem, vmem],
        out_specs=(hbm, hbm, hbm),
        scratch_shapes=[
            pltpu.VMEM((ROWS, width), F32),
            pltpu.VMEM((RANK, ROWS), F32),
            pltpu.SMEM((1, 2), F32),
            pltpu.SemaphoreType.DMA((2 * CHUNKS + 2,)),
        ],
        compiler_params=limit,
    )(back, half, right)
    return weights, jnp.swapaxes(state, 1, 2), consensus[0], norms


def solution(mesh):
    finer = Mesh(
        mesh.devices.reshape(4, 4, 2, 2, 4), ("gossip_0", "gossip_1", "gossip_2", "mp_0", "mp_1")
    )
    gossip = ("gossip_0", "gossip_1", "gossip_2")
    mp = ("mp_0", "mp_1")
    return jax.shard_map(
        body,
        mesh=finer,
        in_specs=(P(gossip, None, mp), P(gossip, None, None), P(None, gossip, None, mp), P(mp, None), P(None, gossip)),
        out_specs=(P(gossip, None, mp), P(gossip, None, None), P(), P()),
        check_vma=False,
    )
```
